256 devices in a mesh: dir: 16 (over y_lo, x, core), box: 16 (over z, y_hi).
Axes of the slice: x: 4, y: 4 (y_hi: 2, y_lo: 2; y = y_hi * 2 + y_lo), z: 8, core: 2. Of those that a mesh axis runs over, the one named last changes fastest.
Arguments:
- child_patterns: float32 [2, 128, 8, 128, 256], P(None, 'box', None, 'dir'), may hold values from -6 to 6
- translation: float32 [32, 2, 256, 512], P(None, None, 'dir'), may hold values from -1.5 to 1.5
- source_list: int32 [128, 24], P('box'), may hold values from -1 to 127, as said below
- operator_list: int32 [128, 24], P('box'), may hold values from 0 to 31
Outputs:
- incoming: float32 [2, 128, 8, 128, 256], P(None, 'box', None, 'dir')
The draws below stay inside these ranges and needn't reach their ends.
Inputs may be any that keep to these rules, and one draw needn't show every extreme that they name: `source_list`: each row names distinct boxes other than the row's own box, then -1 in every unused entry; at least one row is full.
All inputs are finite; a program needn't handle non-finite values.
Results may differ from the reference program's by a relative error of at most 0.0003.
Values sent between devices are 32-bit elements; how exact they have to be, the bound alone decides.
No kernel may reach another device: no remote copies, remote signals or barrier semaphores. Data moves between devices by JAX's collectives and lax.ppermute only.
A program may use at most 192 MiB of HBM per device.

```python
import jax
import jax.numpy as jnp
from jax import lax

LIST = 24
NOPS = 32
BOXES = 128
PT = 256
PP = 512
CT = 128
CP = 256


def draw_source_list(key, part):
    key = jax.random.fold_in(key, 11)
    score_key, length_key, full_key = jax.random.split(key, 3)
    box_ids = jnp.arange(BOXES, dtype=jnp.int32)
    scores = jax.random.randint(score_key, (BOXES, BOXES), 0, 2 ** 20, dtype=jnp.int32) * BOXES + box_ids[None, :]
    scores = jnp.where(box_ids[:, None] == box_ids[None, :], jnp.int32(2 ** 30), scores)
    ordered = jnp.argsort(scores, axis=1)[:, :LIST].astype(jnp.int32)
    lengths = jax.random.randint(length_key, (BOXES,), 1, LIST + 1, dtype=jnp.int32)
    full_row = jax.random.randint(full_key, (), 0, BOXES, dtype=jnp.int32)
    lengths = jnp.where(box_ids == full_row, jnp.int32(LIST), lengths)
    used = jnp.arange(LIST, dtype=jnp.int32)[None, :] < lengths[:, None]
    return jnp.where(used, ordered, jnp.int32(-1)).astype(jnp.int32)


def with_ends(entries, rng, smallest, top_value):
    shape = entries.shape
    index_at = [jax.random.randint(jax.random.fold_in(rng, axis), (), 0, shape[axis]) for axis in range(len(shape))]
    entries = entries.at[tuple(index_at)].set(smallest)
    longest = shape.index(max(shape))
    index_at[longest] = (index_at[longest] + 1) % shape[longest]
    return entries.at[tuple(index_at)].set(top_value)


def block_scale(own_key, dims, pieces, smallest, high):
    loudness, own = 1.0, jax.random.fold_in(own_key, 6)
    for dim, parts in pieces:
        heights = jnp.exp(jax.random.uniform(jax.random.fold_in(own, dim), (parts,), jnp.float32, smallest / len(pieces), high / len(pieces)))
        loudness = loudness * jnp.repeat(heights, dims[dim] // parts).reshape([-1 if axis == dim else 1 for axis in range(len(dims))])
    return loudness


def gaussian(key, shape, width, most, shards=(), held_as=jnp.bfloat16):
    entries = width * jax.random.normal(key, shape, jnp.float32)
    if shards:
        entries = entries * block_scale(key, shape, shards, -0.22, 0.18)
    return jnp.clip(entries, -most, most).astype(held_as)


def setup_inputs(seed: int = 0) -> dict:
    key_of = jax.random.split(jax.random.key(seed), 5)
    child_patterns = gaussian(key_of[0], (2, BOXES, 8, CT, CP), 1.0, 6.0, ((1, 16), (3, 16)), jnp.float32)
    translation = gaussian(key_of[1], (NOPS, 2, PT, PP), 0.1, 1.5, ((2, 16),), jnp.float32)
    source_list = draw_source_list(jax.random.fold_in(key_of[4], 71), 0)
    operator_list = with_ends(jax.random.randint(key_of[3], (BOXES, LIST), 0, NOPS), jax.random.fold_in(key_of[3], 1), 0, NOPS - 1).astype(jnp.int32)
    return dict(child_patterns=child_patterns, translation=translation, source_list=source_list, operator_list=operator_list)


theta_even = (-0.0390625, 0.2734375, 0.8203125, -0.0546875)
theta_odd = (-0.0546875, 0.8203125, 0.2734375, -0.0390625)
phi_edge = -0.0625
phi_middle = 0.5625


def interp_theta(padded):
    row_count = padded.shape[-2] - 4
    even_rows = sum(theta_even[offset] * padded[..., offset:offset + row_count, :] for offset in range(4))
    odd_rows = sum(theta_odd[offset] * padded[..., offset + 1:offset + 1 + row_count, :] for offset in range(4))
    stacked = jnp.stack([even_rows, odd_rows], axis=-2)
    return stacked.reshape(stacked.shape[:-3] + (2 * row_count, stacked.shape[-1]))


def interp_phi(values):
    odd_cols = phi_edge * jnp.roll(values, 1, axis=-1) + phi_middle * values + phi_middle * jnp.roll(values, -1, axis=-1) + phi_edge * jnp.roll(values, -2, axis=-1)
    stacked = jnp.stack([values, odd_cols], axis=-1)
    return stacked.reshape(stacked.shape[:-2] + (2 * values.shape[-1],))


def anterp_phi(values):
    even_cols = values[..., 0::2]
    odd_cols = values[..., 1::2]
    return even_cols + phi_edge * jnp.roll(odd_cols, -1, axis=-1) + phi_middle * odd_cols + phi_middle * jnp.roll(odd_cols, 1, axis=-1) + phi_edge * jnp.roll(odd_cols, 2, axis=-1)


def anterp_theta(padded):
    row_count = (padded.shape[-2] - 6) // 2
    even_part = padded[..., 1::2, :]
    odd_part = padded[..., 0::2, :]
    return sum(theta_even[offset] * even_part[..., 3 - offset:3 - offset + row_count, :] + theta_odd[offset] * odd_part[..., 3 - offset:3 - offset + row_count, :] for offset in range(4))


def phases(row_index, total_rows, total_cols):
    polar = (row_index.astype(jnp.float32) + 0.5) * (jnp.pi / total_rows)
    azimuth = jnp.arange(total_cols, dtype=jnp.float32) * (2.0 * jnp.pi / total_cols)
    octant = jnp.arange(8, dtype=jnp.int32)
    sign_x = ((octant % 2) * 2 - 1).astype(jnp.float32)[:, None, None]
    sign_y = (((octant // 2) % 2) * 2 - 1).astype(jnp.float32)[:, None, None]
    sign_z = ((octant // 4) * 2 - 1).astype(jnp.float32)[:, None, None]
    wave_size = 0.125 * total_rows
    sin_polar = jnp.sin(polar)[None, :, None]
    cos_polar = jnp.cos(polar)[None, :, None]
    angle_table = wave_size * (sign_x * sin_polar * jnp.cos(azimuth)[None, None, :] + sign_y * sin_polar * jnp.sin(azimuth)[None, None, :] + sign_z * cos_polar)
    return jnp.cos(angle_table), jnp.sin(angle_table)


def reference(child_patterns, translation, source_list, operator_list):
    child_rows = child_patterns.shape[3]
    total_rows = 2 * child_rows
    total_cols = 2 * child_patterns.shape[4]
    cosine, sine_part = phases(jnp.arange(total_rows, dtype=jnp.int32), total_rows, total_cols)

    def aggregate(one_box):
        padded = jnp.pad(one_box, ((0, 0), (0, 0), (2, 2), (0, 0)))
        refined = interp_phi(interp_theta(padded))
        real_part = refined[0] * cosine + refined[1] * sine_part
        imag_part = refined[1] * cosine - refined[0] * sine_part
        return jnp.stack([jnp.sum(real_part, axis=0), jnp.sum(imag_part, axis=0)])

    parent = lax.map(aggregate, jnp.moveaxis(child_patterns, 1, 0))

    def add_entry(total_field, columns):
        sources, operators = columns
        valid = sources >= 0
        pattern = parent[jnp.maximum(sources, 0)]
        chosen = translation[operators]
        real_part = chosen[:, 0] * pattern[:, 0] - chosen[:, 1] * pattern[:, 1]
        imag_part = chosen[:, 0] * pattern[:, 1] + chosen[:, 1] * pattern[:, 0]
        term = jnp.stack([real_part, imag_part], axis=1)
        return total_field + jnp.where(valid[:, None, None, None], term, jnp.float32(0.0)), None

    received, _ = lax.scan(add_entry, jnp.zeros(parent.shape, jnp.float32), (source_list.T, operator_list.T))

    def disaggregate(one_box):
        real_part = one_box[0][None] * cosine - one_box[1][None] * sine_part
        imag_part = one_box[1][None] * cosine + one_box[0][None] * sine_part
        shifted = anterp_phi(jnp.stack([real_part, imag_part]))
        padded = jnp.pad(shifted, ((0, 0), (0, 0), (3, 3), (0, 0)))
        return anterp_theta(padded)

    incoming = lax.map(disaggregate, received)
    return jnp.moveaxis(incoming, 0, 1)
```

```python
import functools

import jax
import jax.numpy as jnp
from jax import lax
from jax.experimental import pallas as pl
from jax.experimental.pallas import tpu as pltpu
from jax.sharding import PartitionSpec as P

TAP = {
    -3: -0.0390625,
    -2: -0.0546875,
    -1: 0.2734375,
    0: 0.8203125,
    1: 0.8203125,
    2: 0.2734375,
    3: -0.0546875,
    4: -0.0390625,
}
KIDS = 8
HALO = 3
LANES = 128
CHUNK = 8
VMEM = 24 * 1024 * 1024


def tile_iota():
    sub = lax.broadcasted_iota(jnp.int32, (8, LANES), 0)
    lane = lax.broadcasted_iota(jnp.int32, (8, LANES), 1)
    return sub, lane


def swap_parts(tile):
    return jnp.concatenate([tile[4:8], tile[0:4]], axis=0)


def fill_phases(table, rows, first_row, total_rows, total_cols):
    sub, lane = tile_iota()
    block = sub % 4
    sample = 2 * ((block % 2) * LANES + lane) + block // 2
    azimuth = sample.astype(jnp.float32) * (2.0 * jnp.pi / total_cols)
    low = sub < 4
    course = jnp.where(low, jnp.cos(azimuth), jnp.sin(azimuth))
    wave = 0.125 * total_rows
    padded = -(-len(rows) // 8) * 8
    offset = lax.broadcasted_iota(jnp.int32, (padded, LANES), 0)
    number = jnp.zeros((padded, LANES), jnp.int32)
    for i, r in enumerate(rows):
        number = jnp.where(offset == i, r, number)
    polar = ((number + first_row).astype(jnp.float32) + 0.5) * (jnp.pi / total_rows)
    sin_polar = wave * jnp.sin(polar)
    height = wave * jnp.cos(polar)
    cos_z = jnp.cos(height)
    sin_z = jnp.sin(height)
    for i in range(len(rows)):
        angle = sin_polar[i : i + 1] * course
        cos_a, sin_a = jnp.cos(angle), jnp.sin(angle)
        cos_b, sin_b = swap_parts(cos_a), swap_parts(sin_a)
        cx, cy = jnp.where(low, cos_a, cos_b), jnp.where(low, cos_b, cos_a)
        sx, sy = jnp.where(low, sin_a, sin_b), jnp.where(low, sin_b, sin_a)
        cc, ss, sc, cs = cx * cy, sx * sy, sx * cy, cx * sy
        plus_c, plus_s = cc - ss, sc + cs
        minus_c, minus_s = cc + ss, sc - cs
        cz, sz = cos_z[i : i + 1], sin_z[i : i + 1]
        for p in range(4):
            x_up, y_up = p % 2 == 1, p // 2 == 1
            base_c, base_s = (plus_c, plus_s) if x_up == y_up else (minus_c, minus_s)
            if not x_up:
                base_s = -base_s
            at = (i * 4 + p) * 16
            table[at : at + 8, :] = base_c * cz - base_s * sz
            table[at + 8 : at + 16, :] = base_s * cz + base_c * sz


def azimuth_weights(cols, transpose):
    i = lax.broadcasted_iota(jnp.int32, (cols, cols), 0)
    j = lax.broadcasted_iota(jnp.int32, (cols, cols), 1)
    shift = (j - i if transpose else i - j) % cols
    near = (shift == 0) | (shift == 1)
    far = (shift == cols - 1) | (shift == 2)
    return jnp.where(near, 0.5625, jnp.where(far, -0.0625, 0.0)).astype(jnp.bfloat16)


def split_dot(values, weights):
    high = values.astype(jnp.bfloat16)
    rest = (values - high.astype(jnp.float32)).astype(jnp.bfloat16)
    both = jnp.concatenate([high, rest], axis=0)
    out = jnp.dot(both, weights, preferred_element_type=jnp.float32)
    count = values.shape[0]
    return out[:count] + out[count:]


def weighted(terms):
    total = None
    for coef, tile in terms:
        part = coef * tile
        total = part if total is None else total + part
    return total


def aggregate(x_ref, tiles, table, rows, first_row, total_rows, total_cols, store):
    boxes = x_ref.shape[1] // 64
    cols = x_ref.shape[2]
    fill_phases(table, rows, first_row, total_rows, total_cols)
    weights = azimuth_weights(cols, False)
    sub, _ = tile_iota()
    sign = jnp.where(sub < 4, 1.0, -1.0).astype(jnp.float32)

    def refine(b, carry):
        parts = []
        for part in range(2):
            kids = [x_ref[part, pl.ds(pl.multiple_of(b * 64 + c * 8, 8), 8), :] for c in range(KIDS)]
            both = [kids[4 + p] + kids[3 - p] for p in range(4)]
            both += [kids[4 + p] - kids[3 - p] for p in range(4)]
            parts.append(jnp.concatenate(both, axis=0))
        even = jnp.concatenate(parts, axis=0)
        odd = split_dot(even, weights)
        for part in range(2):
            for block in range(4):
                source = even if block < 2 else odd
                lanes = slice((block % 2) * LANES, (block % 2 + 1) * LANES)
                tiles[pl.ds(b * 512 + part * 4 + block, 64, stride=8), :] = source[
                    part * 64 : part * 64 + 64, lanes
                ]
        return carry

    lax.fori_loop(0, boxes, refine, 0)

    def combine(b, carry):
        for i, r in enumerate(rows):
            taps = [(TAP[r - 2 * k], k) for k in range(8) if r - 2 * k in TAP]
            total, turned = None, None
            for p in range(4):
                sums = []
                for q in (p, 4 + p):
                    sums.append(
                        weighted(
                            [
                                (
                                    coef,
                                    tiles[pl.ds(pl.multiple_of(b * 512 + (q * 8 + k) * 8, 8), 8), :],
                                )
                                for coef, k in taps
                            ]
                        )
                    )
                at = (i * 4 + p) * 16
                first = sums[0] * table[at : at + 8, :]
                second = sums[1] * table[at + 8 : at + 16, :]
                total = first if total is None else total + first
                turned = second if turned is None else turned + second
            store(i, b, total + swap_parts(turned) * sign)
        return carry

    lax.fori_loop(0, boxes, combine, 0)


def halo_kernel(total_rows, total_cols, x_ref, up_ref, down_ref, tiles, table):
    first_row = lax.axis_index("dir") * 16

    def store(i, b, tile):
        ref = up_ref if i < HALO else down_ref
        ref[pl.ds(pl.multiple_of((i % HALO) * 64 + b * 8, 8), 8), :] = tile

    rows = (-3, -2, -1, 16, 17, 18)
    aggregate(x_ref, tiles, table, rows, first_row, total_rows, total_cols, store)


def main_kernel(
    total_rows, total_cols, x_ref, note_ref, row_ref, out_ref, operator_ref, tiles, table
):
    first_row = lax.axis_index("dir") * 16

    def store(i, b, tile):
        out_ref[pl.ds(pl.multiple_of(i * 72 + b * 8, 8), 8), :] = tile

    aggregate(x_ref, tiles, table, tuple(range(16)), first_row, total_rows, total_cols, store)
    for r in range(16):
        out_ref[r * 72 + 64 : r * 72 + 72, :] = note_ref[...]
    count = row_ref.shape[0]
    wide = row_ref.shape[1]
    source = lax.broadcasted_iota(jnp.int32, (wide, wide), 0)
    target = lax.broadcasted_iota(jnp.int32, (wide, wide), 1)
    half = wide // 2
    wanted = jnp.where(target < half, 2 * target, 2 * (target - half) + 1)
    pick = jnp.where(source == wanted, 1.0, 0.0).astype(jnp.bfloat16)
    values = row_ref[...]
    high = values.astype(jnp.bfloat16)
    rest = values - high.astype(jnp.float32)
    middle = rest.astype(jnp.bfloat16)
    low = (rest - middle.astype(jnp.float32)).astype(jnp.bfloat16)
    three = jnp.dot(
        jnp.concatenate([high, middle, low], axis=0), pick, preferred_element_type=jnp.float32
    )
    sorted_row = three[:count] + three[count : 2 * count] + three[2 * count :]
    for block in range(4):
        part = sorted_row[:, block * LANES : (block + 1) * LANES]
        operator_ref[pl.ds(block, count, stride=8), :] = part
        operator_ref[pl.ds(block + 4, count, stride=8), :] = part
    operator_ref[count * 8 : count * 8 + 16, :] = jnp.zeros((16, LANES), jnp.float32)


def translate_kernel(x_ref, operator_ref, out_ref, notes, scalars, sem):
    groups = out_ref.shape[0] // 64
    for g in range(groups):
        notes[g * 4 : g * 4 + 4, :] = x_ref[g * 72 + 64 : g * 72 + 68, :].astype(jnp.int32)
    copy = pltpu.make_async_copy(notes, scalars, sem)
    copy.start()
    copy.wait()
    sub, _ = tile_iota()
    sign = jnp.where(sub < 4, -1.0, 1.0).astype(jnp.float32)
    zero = jnp.zeros((8, LANES), jnp.float32)

    def group(g, carry):
        for b in range(8):

            def step(c, sums):
                total, turned = sums
                entry = b * 24 + c * CHUNK
                row, lane = g * 4 + entry // LANES, entry % LANES
                firsts, seconds = [], []
                for k in range(CHUNK):
                    at = pl.multiple_of(scalars[row, lane + k], 8)
                    by = pl.multiple_of(scalars[row + 2, lane + k], 8)
                    pattern = x_ref[pl.ds(at, 8), :]
                    firsts.append(pattern * operator_ref[pl.ds(by, 8), :])
                    seconds.append(pattern * operator_ref[pl.ds(by + 8, 8), :])
                while len(firsts) > 1:
                    firsts = [m + n for m, n in zip(firsts[::2], firsts[1::2])]
                    seconds = [m + n for m, n in zip(seconds[::2], seconds[1::2])]
                return total + firsts[0], turned + seconds[0]

            steps = scalars[g * 4 + 1, 64 + b]
            total, turned = lax.fori_loop(0, steps, step, (zero, zero))
            out_ref[pl.ds(pl.multiple_of(g * 64 + b * 8, 8), 8), :] = (
                total + swap_parts(turned) * sign
            )
        return carry

    lax.fori_loop(0, groups, group, 0)


def disaggregate(get_row, boxes, cols, tiles, table, rows, first_row, sizes, store):
    fill_phases(table, rows, first_row, *sizes)
    weights = azimuth_weights(cols, True)
    sub, _ = tile_iota()
    sign = jnp.where(sub < 4, -1.0, 1.0).astype(jnp.float32)
    zero = jnp.zeros((8, LANES), jnp.float32)

    def shift(b, carry):
        plain = [get_row(i, b) for i in range(len(rows))]
        turned = [swap_parts(tile) * sign for tile in plain]
        for p in range(4):
            sums = []
            for which, source in enumerate((plain, turned)):
                product = []
                for i in range(len(rows)):
                    at = (i * 4 + p) * 16 + which * 8
                    product.append(source[i] * table[at : at + 8, :])
                per_row = []
                for k in range(8):
                    terms = [
                        (TAP[r - 2 * k], product[i]) for i, r in enumerate(rows) if r - 2 * k in TAP
                    ]
                    per_row.append(weighted(terms) if terms else None)
                sums.append(per_row)
            for k in range(8):
                for c, scale in ((4 + p, 1.0), (3 - p, -1.0)):
                    if sums[0][k] is None:
                        tile = zero
                    else:
                        tile = sums[0][k] + sums[1][k] if scale > 0 else sums[0][k] - sums[1][k]
                    at = pl.multiple_of(b * 512 + (c * 8 + k) * 8, 8)
                    tiles[pl.ds(at, 8), :] = tile
        return carry

    lax.fori_loop(0, boxes, shift, 0)

    def gather(b, carry):
        even, odd = [], []
        for part in range(2):
            blocks = [tiles[pl.ds(b * 512 + part * 4 + block, 64, stride=8), :] for block in range(4)]
            even.append(jnp.concatenate(blocks[:2], axis=1))
            odd.append(jnp.concatenate(blocks[2:], axis=1))
        mixed = split_dot(jnp.concatenate(odd, axis=0), weights)
        for part in range(2):
            store(part, b, even[part] + mixed[part * 64 : part * 64 + 64])
        return carry

    lax.fori_loop(0, boxes, gather, 0)


def inner_kernel(sizes, r_ref, out_ref, tiles, table):
    def get_row(i, b):
        return r_ref[pl.ds(pl.multiple_of(i * 64 + b * 8, 8), 8), :]

    def store(part, b, value):
        out_ref[part, pl.ds(pl.multiple_of(b * 64, 8), 64), :] = value

    first_row = lax.axis_index("dir") * 16
    boxes, cols = out_ref.shape[1] // 64, out_ref.shape[2]
    rows = tuple(range(16))
    disaggregate(get_row, boxes, cols, tiles, table, rows, first_row, sizes, store)


def outer_kernel(sizes, before_ref, after_ref, part_ref, out_ref, tiles, table):
    def get_row(i, b):
        ref = before_ref if i < HALO else after_ref
        return ref[pl.ds(pl.multiple_of((i % HALO) * 64 + b * 8, 8), 8), :]

    def store(part, b, value):
        at = pl.ds(pl.multiple_of(b * 64, 8), 64)
        out_ref[part, at, :] = part_ref[part, at, :] + value

    first_row = lax.axis_index("dir") * 16
    boxes, cols = out_ref.shape[1] // 64, out_ref.shape[2]
    rows = (-3, -2, -1, 16, 17, 18)
    disaggregate(get_row, boxes, cols, tiles, table, rows, first_row, sizes, store)


def neighbours(upward, downward):
    size = lax.axis_size("dir")
    to_next = [(i, i + 1) for i in range(size - 1)]
    to_last = [(i + 1, i) for i in range(size - 1)]
    return lax.ppermute(upward, "dir", to_next), lax.ppermute(downward, "dir", to_last)


def call(kernel, outs, scratch, flops, moved, *args):
    return pl.pallas_call(
        kernel,
        out_shape=outs,
        scratch_shapes=scratch,
        compiler_params=pltpu.CompilerParams(vmem_limit_bytes=VMEM),
        cost_estimate=pl.CostEstimate(flops=flops, bytes_accessed=moved, transcendentals=0),
    )(*args)


def list_notes(source_list, operator_list, operators):
    boxes = source_list.shape[0]
    used = source_list >= 0
    at = jnp.where(used, (source_list + source_list // boxes) * 8, 0)
    by = jnp.where(used, operator_list, operators) * 16
    steps = (jnp.sum(used.astype(jnp.int32), axis=1) + CHUNK - 1) // CHUNK
    at = jnp.concatenate([at.reshape(-1), steps, jnp.zeros((56,), jnp.int32)])
    by = jnp.concatenate([by.reshape(-1), jnp.zeros((64,), jnp.int32)])
    notes = jnp.concatenate([at, by, jnp.zeros((512,), jnp.int32)])
    return notes.reshape(8, LANES).astype(jnp.float32)


def on_device(child_patterns, translation, source_list, operator_list):
    parts, boxes, kids, half_rows, cols = child_patterns.shape
    local_rows = 2 * half_rows
    sizes = (local_rows * lax.axis_size("dir"), 2 * cols)
    groups = lax.axis_size("box")
    operators = translation.shape[0]
    f32 = jnp.float32
    shape = jax.ShapeDtypeStruct
    x = child_patterns.reshape(parts, boxes * kids * half_rows, cols)
    work = pltpu.VMEM((boxes * 512, LANES), f32)

    def phase_table(rows):
        return pltpu.VMEM((rows * 64, LANES), f32)

    up, down = call(
        functools.partial(halo_kernel, *sizes),
        [shape((HALO * boxes * 8, LANES), f32)] * 2,
        [work, phase_table(2 * HALO)],
        10**7,
        10**6,
        x,
    )
    before, after = neighbours(down, up)
    notes = list_notes(source_list, operator_list, operators)
    row = lax.dynamic_index_in_dim(translation, lax.axis_index("box"), 2, keepdims=False)
    row = row.reshape(operators * 2, 2 * cols)
    own, sorted_operators = call(
        functools.partial(main_kernel, *sizes),
        [
            shape((local_rows * 72, LANES), f32),
            shape(((operators + 1) * 16, LANES), f32),
        ],
        [work, phase_table(local_rows)],
        2 * 10**7,
        4 * 10**6,
        x,
        notes,
        row,
    )
    own = own.reshape(local_rows, 72, LANES)
    extra = ((0, 0), (0, 8), (0, 0))
    before = jnp.pad(before.reshape(HALO, 64, LANES), extra)
    after = jnp.pad(after.reshape(HALO, 64, LANES), extra)
    parent = jnp.concatenate([own[:HALO] + before, own[HALO:-HALO], own[-HALO:] + after])
    patterns = lax.all_to_all(parent, "box", 0, 0, tiled=True)
    received = call(
        translate_kernel,
        shape((groups * 64, LANES), f32),
        [
            pltpu.VMEM((groups * 4, LANES), jnp.int32),
            pltpu.SMEM((groups * 4, LANES), jnp.int32),
            pltpu.SemaphoreType.DMA,
        ],
        2 * 10**7,
        2 * 10**6,
        patterns.reshape(groups * 72, LANES),
        sorted_operators,
    )
    received = received.reshape(groups, 64, LANES)
    received = lax.all_to_all(received, "box", 0, 0, tiled=True)
    received = received.reshape(local_rows * 64, LANES)
    edge = HALO * 64
    before, after = neighbours(received[-edge:], received[:edge])
    out_shape = shape((parts, boxes * kids * half_rows, cols), f32)
    inner = call(
        functools.partial(inner_kernel, sizes),
        out_shape,
        [work, phase_table(local_rows)],
        2 * 10**7,
        4 * 10**6,
        received,
    )
    out = call(
        functools.partial(outer_kernel, sizes),
        out_shape,
        [work, phase_table(2 * HALO)],
        10**7,
        2 * 10**6,
        before,
        after,
        inner,
    )
    return out.reshape(child_patterns.shape)


def solution(mesh):
    return jax.shard_map(
        on_device,
        mesh=mesh,
        in_specs=(
            P(None, "box", None, "dir", None),
            P(None, None, "dir", None),
            P("box", None),
            P("box", None),
        ),
        out_specs=P(None, "box", None, "dir", None),
        check_vma=False,
    )
```

```python
import functools

import jax
import jax.numpy as jnp
from jax import lax
from jax.experimental import pallas as pl
from jax.experimental.pallas import tpu as pltpu
from jax.sharding import PartitionSpec as P

TAP = {
    -3: -0.0390625,
    -2: -0.0546875,
    -1: 0.2734375,
    0: 0.8203125,
    1: 0.8203125,
    2: 0.2734375,
    3: -0.0546875,
    4: -0.0390625,
}
KIDS = 8
HALO = 3
LANES = 128
OPERATORS = 32
MAIN_ROWS = tuple(range(-3, 13))
EDGE_ROWS = tuple(range(13, 19))
VMEM = 24 * 1024 * 1024
PICK_VMEM = 61_500_000


def tile_iota():
    sub = lax.broadcasted_iota(jnp.int32, (8, LANES), 0)
    lane = lax.broadcasted_iota(jnp.int32, (8, LANES), 1)
    return sub, lane


def swap_parts(tile):
    return jnp.concatenate([tile[4:8], tile[0:4]], axis=0)


def sin_cos(angle):
    quarter = jnp.floor(angle * (2.0 / jnp.pi) + 0.5)
    rest = angle - quarter * 1.5703125
    rest = rest - quarter * 4.837512969970703125e-4
    rest = rest - quarter * 7.54978995489188e-8
    square = rest * rest
    sine = -1.9515295891e-4 * square + 8.3321608736e-3
    sine = (sine * square - 1.6666654611e-1) * square * rest + rest
    cosine = 2.443315711809948e-5 * square - 1.388731625493765e-3
    cosine = (cosine * square + 4.166664568298827e-2) * square * square - 0.5 * square + 1.0
    number = quarter.astype(jnp.int32)
    odd = (number & 1) == 1
    first, second = jnp.where(odd, cosine, sine), jnp.where(odd, sine, cosine)
    first = jnp.where((number & 2) == 2, -first, first)
    second = jnp.where(((number + 1) & 2) == 2, -second, second)
    return first, second


def fill_phases(table, rows, first_row, total_rows, total_cols):
    sub, lane = tile_iota()
    block = sub % 4
    sample = 2 * ((block % 2) * LANES + lane) + block // 2
    azimuth = sample.astype(jnp.float32) * (2.0 * jnp.pi / total_cols)
    low = sub < 4
    sin_azimuth, cos_azimuth = sin_cos(azimuth)
    course = jnp.where(low, cos_azimuth, sin_azimuth)
    wave = 0.125 * total_rows
    padded = -(-len(rows) // 8) * 8
    number = lax.broadcasted_iota(jnp.int32, (padded, LANES), 0) + (first_row + rows[0])
    inside = (number >= 0) & (number < total_rows)
    polar = (number.astype(jnp.float32) + 0.5) * (jnp.pi / total_rows)
    sin_polar, cos_polar = sin_cos(polar)
    sin_z, cos_z = sin_cos(wave * cos_polar)
    sin_polar = wave * sin_polar
    cos_z, sin_z = jnp.where(inside, cos_z, 0.0), jnp.where(inside, sin_z, 0.0)
    for i in range(len(rows)):
        sin_a, cos_a = sin_cos(sin_polar[i : i + 1] * course)
        cos_b, sin_b = swap_parts(cos_a), swap_parts(sin_a)
        cx, cy = jnp.where(low, cos_a, cos_b), jnp.where(low, cos_b, cos_a)
        sx, sy = jnp.where(low, sin_a, sin_b), jnp.where(low, sin_b, sin_a)
        cc, ss, sc, cs = cx * cy, sx * sy, sx * cy, cx * sy
        plus_c, plus_s = cc - ss, sc + cs
        minus_c, minus_s = cc + ss, sc - cs
        cz, sz = cos_z[i : i + 1], sin_z[i : i + 1]
        for p in range(4):
            x_up, y_up = p % 2 == 1, p // 2 == 1
            base_c, base_s = (plus_c, plus_s) if x_up == y_up else (minus_c, minus_s)
            if not x_up:
                base_s = -base_s
            at = (i * 4 + p) * 16
            table[at : at + 8, :] = base_c * cz - base_s * sz
            table[at + 8 : at + 16, :] = base_s * cz + base_c * sz


def azimuth_weights(cols, transpose):
    i = lax.broadcasted_iota(jnp.int32, (cols, cols), 0)
    j = lax.broadcasted_iota(jnp.int32, (cols, cols), 1)
    shift = (j - i if transpose else i - j) % cols
    near = (shift == 0) | (shift == 1)
    far = (shift == cols - 1) | (shift == 2)
    return jnp.where(near, 0.5625, jnp.where(far, -0.0625, 0.0)).astype(jnp.bfloat16)


def split_dot(values, weights):
    high = values.astype(jnp.bfloat16)
    rest = (values - high.astype(jnp.float32)).astype(jnp.bfloat16)
    both = jnp.concatenate([high, rest], axis=0)
    out = jnp.dot(both, weights, preferred_element_type=jnp.float32)
    count = values.shape[0]
    return out[:count] + out[count:]


def weighted(terms):
    total = None
    for coef, tile in terms:
        part = coef * tile
        total = part if total is None else total + part
    return total


def aggregate(x_ref, tiles, table, rows, store):
    boxes = x_ref.shape[1] // 64
    weights = azimuth_weights(x_ref.shape[2], False)
    sub, _ = tile_iota()
    sign = jnp.where(sub < 4, 1.0, -1.0).astype(jnp.float32)

    def refine(b):
        parts = []
        for part in range(2):
            kids = [x_ref[part, pl.ds(pl.multiple_of(b * 64 + c * 8, 8), 8), :] for c in range(KIDS)]
            both = [kids[4 + p] + kids[3 - p] for p in range(4)]
            both += [kids[4 + p] - kids[3 - p] for p in range(4)]
            parts.append(jnp.concatenate(both, axis=0))
        even = jnp.concatenate(parts, axis=0)
        odd = split_dot(even, weights)
        for part in range(2):
            for block in range(4):
                source = even if block < 2 else odd
                lanes = slice((block % 2) * LANES, (block % 2 + 1) * LANES)
                tiles[pl.ds(b * 512 + part * 4 + block, 64, stride=8), :] = source[
                    part * 64 : part * 64 + 64, lanes
                ]

    def combine(b):
        for i, r in enumerate(rows):
            taps = [(TAP[r - 2 * k], k) for k in range(8) if r - 2 * k in TAP]
            total, turned = None, None
            for p in range(4):
                sums = []
                for q in (p, 4 + p):
                    parts = []
                    for coef, k in taps:
                        at = pl.multiple_of(b * 512 + (q * 8 + k) * 8, 8)
                        parts.append((coef, tiles[pl.ds(at, 8), :]))
                    sums.append(weighted(parts))
                at = (i * 4 + p) * 16
                first = sums[0] * table[at : at + 8, :]
                second = sums[1] * table[at + 8 : at + 16, :]
                total = first if total is None else total + first
                turned = second if turned is None else turned + second
            store(i, b, total + swap_parts(turned) * sign)

    def box(b, carry):
        refine(b)
        combine(b)
        return carry

    lax.fori_loop(0, boxes, box, 0, unroll=2)


def edge_kernel(sizes, x_ref, out_ref, table, tiles):
    fill_phases(table, EDGE_ROWS, lax.axis_index("dir") * 16, *sizes)

    def store(i, b, tile):
        out_ref[pl.ds(pl.multiple_of(i * 64 + b * 8, 8), 8), :] = tile

    aggregate(x_ref, tiles, table, EDGE_ROWS, store)


def main_kernel(sizes, x_ref, source_ref, list_ref, out_ref, table, tiles):
    fill_phases(table, MAIN_ROWS, lax.axis_index("dir") * 16, *sizes)

    def store(i, b, tile):
        out_ref[pl.ds(pl.multiple_of(i * 72 + b * 8, 8), 8), :] = tile

    aggregate(x_ref, tiles, table, MAIN_ROWS, store)
    boxes, entries = source_ref.shape
    source = source_ref[...]
    used = source >= 0
    at = jnp.where(used, (source + source // boxes) * 8, 0)
    by = jnp.where(used, list_ref[...], OPERATORS) * 16
    out_ref[64:72, :] = jnp.zeros((8, LANES), jnp.float32)
    out_ref[64:72, 0:entries] = at.astype(jnp.float32)
    out_ref[64:72, 32 : 32 + entries] = by.astype(jnp.float32)
    note = out_ref[64:72, :]
    for r in range(1, len(MAIN_ROWS)):
        out_ref[r * 72 + 64 : r * 72 + 72, :] = note


def join_kernel(own_ref, edge_ref, out_ref):
    count = len(EDGE_ROWS)
    for i in range(count):
        out_ref[i * 72 : i * 72 + 64, :] = (
            own_ref[i * 72 : i * 72 + 64, :] + edge_ref[i * 64 : i * 64 + 64, :]
        )
        out_ref[i * 72 + 64 : i * 72 + 72, :] = own_ref[i * 72 + 64 : i * 72 + 72, :]
    out_ref[count * 72 :, :] = own_ref[count * 72 :, :]


def pick_kernel(all_ref, out_ref, block_ref, sem):
    rows = all_ref.shape[1]
    wanted = (lax.axis_index("box") + rows - HALO) % rows
    near = pl.ds(pl.multiple_of(wanted // 8 * 8, 8), 8)
    copy = pltpu.make_async_copy(all_ref.at[:, near, :], block_ref, sem)
    copy.start()
    copy.wait()
    at = wanted % 8

    def eight(i, carry):
        first = pl.multiple_of(i * 8, 8)
        rows = [block_ref[first + n, pl.ds(at, 1), :] for n in range(8)]
        out_ref[pl.ds(first, 8), :] = jnp.concatenate(rows, axis=0)
        return carry

    lax.fori_loop(0, out_ref.shape[0] // 8, eight, 0)


def sort_kernel(row_ref, out_ref):
    count, wide = row_ref.shape
    source = lax.broadcasted_iota(jnp.int32, (wide, wide), 0)
    target = lax.broadcasted_iota(jnp.int32, (wide, wide), 1)
    half = wide // 2
    wanted = jnp.where(target < half, 2 * target, 2 * (target - half) + 1)
    pick = jnp.where(source == wanted, 1.0, 0.0).astype(jnp.bfloat16)
    values = row_ref[...]
    high = values.astype(jnp.bfloat16)
    rest = values - high.astype(jnp.float32)
    middle = rest.astype(jnp.bfloat16)
    low = (rest - middle.astype(jnp.float32)).astype(jnp.bfloat16)
    three = jnp.dot(
        jnp.concatenate([high, middle, low], axis=0), pick, preferred_element_type=jnp.float32
    )
    in_order = three[:count] + three[count : 2 * count] + three[2 * count :]
    for block in range(4):
        part = in_order[:, block * LANES : (block + 1) * LANES]
        out_ref[pl.ds(block, count, stride=8), :] = part
        out_ref[pl.ds(block + 4, count, stride=8), :] = part
    out_ref[count * 8 : count * 8 + 16, :] = jnp.zeros((16, LANES), jnp.float32)


def translate_kernel(entries, x_ref, operator_ref, out_ref, notes, scalars, sems):
    pairs = out_ref.shape[0] // 128
    sub, lane = tile_iota()
    for h in range(pairs):
        at = h * 144 + 64
        first, second = x_ref[at : at + 8, :], x_ref[at + 72 : at + 80, :]
        both = jnp.where(lane < 64, first, pltpu.roll(second, 64, 1))
        notes[h * 8 : h * 8 + 8, :] = both.astype(jnp.int32)

    def copy(h):
        at = pl.ds(h * 8, 8)
        return pltpu.make_async_copy(notes.at[at, :], scalars.at[at, :], sems.at[h])

    for h in range(pairs):
        copy(h).start()
    sign = jnp.where(sub < 4, -1.0, 1.0).astype(jnp.float32)

    for h in range(pairs):
        copy(h).wait()
        for g in range(2):
            for base in (0, 4):
                sums = [[None, None] for _ in range(4)]
                for k in range(entries):
                    for j in range(4):
                        row = h * 8 + base + j
                        at = pl.multiple_of(scalars[row, g * 64 + k], 8)
                        by = pl.multiple_of(scalars[row, g * 64 + 32 + k], 8)
                        pattern = x_ref[pl.ds(at, 8), :]
                        for which in range(2):
                            part = pattern * operator_ref[pl.ds(by + 8 * which, 8), :]
                            total = sums[j][which]
                            sums[j][which] = part if total is None else total + part
                for j in range(4):
                    at = h * 128 + g * 64 + (base + j) * 8
                    out_ref[at : at + 8, :] = sums[j][0] + swap_parts(sums[j][1]) * sign


def shift_sums(b, get_row, table, rows, kids, sign, put):
    plain = [get_row(i, b) for i in range(len(rows))]
    turned = [swap_parts(tile) * sign for tile in plain]
    for p in range(4):
        sums = []
        for which, source in enumerate((plain, turned)):
            product = []
            for i in range(len(rows)):
                at = (i * 4 + p) * 16 + which * 8
                product.append(source[i] * table[at : at + 8, :])
            per_row = []
            for k in kids:
                terms = [(TAP[r - 2 * k], product[i]) for i, r in enumerate(rows) if r - 2 * k in TAP]
                per_row.append(weighted(terms))
            sums.append(per_row)
        for n, k in enumerate(kids):
            put(4 + p, k, sums[0][n] + sums[1][n])
            put(3 - p, k, sums[0][n] - sums[1][n])


def turn_sign():
    sub, _ = tile_iota()
    return jnp.where(sub < 4, -1.0, 1.0).astype(jnp.float32)


def azimuth_back(tiles, base, rows, weights):
    even, odd = [], []
    for part in range(2):
        blocks = [tiles[pl.ds(base + part * 4 + block, rows, stride=8), :] for block in range(4)]
        even.append(jnp.concatenate(blocks[:2], axis=1))
        odd.append(jnp.concatenate(blocks[2:], axis=1))
    mixed = split_dot(jnp.concatenate(odd, axis=0), weights)
    return [even[part] + mixed[part * rows : part * rows + rows] for part in range(2)]


def inner_kernel(r_ref, table, out_ref, tiles):
    boxes, cols = out_ref.shape[1] // 64, out_ref.shape[2]
    weights = azimuth_weights(cols, True)
    sign = turn_sign()

    def get_row(i, b):
        return r_ref[pl.ds(pl.multiple_of(i * 64 + b * 8, 8), 8), :]

    def shift(b, carry):
        def put(c, k, tile):
            tiles[pl.ds(pl.multiple_of(b * 512 + (c * 8 + k) * 8, 8), 8), :] = tile

        shift_sums(b, get_row, table, MAIN_ROWS, tuple(range(8)), sign, put)
        values = azimuth_back(tiles, b * 512, 64, weights)
        for part in range(2):
            out_ref[part, pl.ds(pl.multiple_of(b * 64, 64), 64), :] = values[part]
        return carry

    lax.fori_loop(0, boxes, shift, 0, unroll=2)


def outer_kernel(edge_ref, table, part_ref, out_hbm, out_ref, tiles, sems):
    boxes, cols = out_ref.shape[1] // 64, out_ref.shape[2]
    weights = azimuth_weights(cols, True)
    sign = turn_sign()
    nothing = jnp.zeros((8, LANES), jnp.float32)

    def get_row(i, b):
        return edge_ref[pl.ds(pl.multiple_of(i * 64 + b * 8, 8), 8), :]

    def copy(part, b):
        at = pl.ds(pl.multiple_of(b * 64, 64), 64)
        return pltpu.make_async_copy(
            out_ref.at[part, at, :], out_hbm.at[part, at, :], sems.at[part, b]
        )

    blank = jnp.zeros((4, cols), jnp.float32)

    def box(b, carry):
        def put(c, k, tile):
            tiles[pl.ds(pl.multiple_of(b * 256 + (c * 4 + k - 4) * 8, 8), 8), :] = tile

        for c in range(KIDS):
            put(c, 4, nothing)
        shift_sums(b, get_row, table, EDGE_ROWS, (5, 6, 7), sign, put)
        values = azimuth_back(tiles, b * 256, 32, weights)
        at = pl.ds(pl.multiple_of(b * 64, 64), 64)
        for part in range(2):
            pieces = []
            for c in range(KIDS):
                pieces += [blank, values[part][c * 4 : c * 4 + 4]]
            out_ref[part, at, :] = part_ref[part, at, :] + jnp.concatenate(pieces, axis=0)
            copy(part, b).start()
        return carry

    lax.fori_loop(0, boxes, box, 0, unroll=2)
    for b in range(boxes):
        for part in range(2):
            copy(part, b).wait()


def to_next(value, step):
    size = lax.axis_size("dir")
    return lax.ppermute(value, "dir", [(i, (i + step) % size) for i in range(size)])


def call(kernel, outs, scratch, flops, moved, *args, in_hbm=(), out_hbm=False, limit=VMEM):
    whole = pl.BlockSpec(memory_space=pltpu.VMEM)
    far = pl.BlockSpec(memory_space=pltpu.HBM)
    out_specs = [whole] * len(outs) if isinstance(outs, list) else far if out_hbm else whole
    return pl.pallas_call(
        kernel,
        out_shape=outs,
        in_specs=[far if i in in_hbm else whole for i in range(len(args))],
        out_specs=out_specs,
        scratch_shapes=scratch,
        compiler_params=pltpu.CompilerParams(vmem_limit_bytes=limit),
        cost_estimate=pl.CostEstimate(flops=flops, bytes_accessed=moved, transcendentals=0),
    )(*args)


def on_device(child_patterns, translation, source_list, operator_list):
    parts, boxes, kids, half_rows, cols = child_patterns.shape
    local_rows = 2 * half_rows
    sizes = (local_rows * lax.axis_size("dir"), 2 * cols)
    groups = lax.axis_size("box")
    operators = translation.shape[0]
    f32 = jnp.float32
    shape = jax.ShapeDtypeStruct
    x = child_patterns.reshape(parts, boxes * kids * half_rows, cols)
    work = pltpu.VMEM((boxes * 512, LANES), f32)
    sems = pltpu.SemaphoreType.DMA((parts, boxes))
    edge = len(EDGE_ROWS)

    share, edge_table = call(
        functools.partial(edge_kernel, sizes),
        [shape((edge * boxes * 8, LANES), f32), shape((edge * 64, LANES), f32)],
        [work],
        10**7,
        10**6,
        x,
    )
    from_last = to_next(share, 1)
    own, main_table = call(
        functools.partial(main_kernel, sizes),
        [shape((local_rows * 72, LANES), f32), shape((local_rows * 64, LANES), f32)],
        [work],
        2 * 10**7,
        4 * 10**6,
        x,
        source_list,
        operator_list,
    )
    parent = call(join_kernel, shape(own.shape, f32), [], 10**5, 10**6, own, from_last)

    parent, translation = lax.optimization_barrier((parent, translation))
    place = lax.axis_index("box")
    row = call(
        pick_kernel,
        shape((operators * 2, 2 * cols), f32),
        [pltpu.VMEM((operators * 2, 8, 2 * cols), f32), pltpu.SemaphoreType.DMA],
        2 * 10**7,
        4 * 10**6,
        translation.reshape(operators * 2, local_rows, 2 * cols),
        in_hbm=(0,),
        limit=PICK_VMEM,
    )
    row = jnp.where(place < HALO, to_next(row, 1), row)
    sorted_operators = call(
        sort_kernel, shape(((operators + 1) * 16, LANES), f32), [], 2 * 10**7, 4 * 10**6, row
    )
    patterns = lax.all_to_all(
        parent.reshape(local_rows, 72, LANES), "box", 0, 0, tiled=True
    ).reshape(groups * 72, LANES)
    received = call(
        functools.partial(translate_kernel, source_list.shape[1]),
        shape((groups * 64, LANES), f32),
        [
            pltpu.VMEM((groups * 4, LANES), jnp.int32),
            pltpu.SMEM((groups * 4, LANES), jnp.int32),
            pltpu.SemaphoreType.DMA((groups // 2,)),
        ],
        2 * 10**7,
        2 * 10**6,
        patterns,
        sorted_operators,
    )
    received = received.reshape(groups, 64, LANES)
    received = lax.all_to_all(received, "box", 0, 0, tiled=True)
    received = received.reshape(local_rows * 64, LANES)
    from_next = to_next(received[: edge * 64], -1)
    inner = call(
        inner_kernel, shape(x.shape, f32), [work], 2 * 10**7, 4 * 10**6, received, main_table
    )
    out = call(
        outer_kernel,
        shape(x.shape, f32),
        [pltpu.VMEM(x.shape, f32), pltpu.VMEM((boxes * 256, LANES), f32), sems],
        10**7,
        2 * 10**6,
        from_next,
        edge_table,
        inner,
        out_hbm=True,
    )
    return out.reshape(child_patterns.shape)


def solution(mesh):
    return jax.shard_map(
        on_device,
        mesh=mesh,
        in_specs=(
            P(None, "box", None, "dir", None),
            P(None, None, "dir", None),
            P("box", None),
            P("box", None),
        ),
        out_specs=P(None, "box", None, "dir", None),
        check_vma=False,
    )
```

```python
import functools

import jax
import jax.numpy as jnp
from jax import lax
from jax.experimental import pallas as pl
from jax.experimental.pallas import tpu as pltpu
from jax.sharding import PartitionSpec as P

TAP = {
    -3: -0.0390625,
    -2: -0.0546875,
    -1: 0.2734375,
    0: 0.8203125,
    1: 0.8203125,
    2: 0.2734375,
    3: -0.0546875,
    4: -0.0390625,
}
KIDS = 8
HALO = 3
LANES = 128
OPERATORS = 32
MAIN_ROWS = tuple(range(-3, 13))
EDGE_ROWS = tuple(range(13, 19))
VMEM = 24 * 1024 * 1024
PICK_VMEM = 61_500_000


def tile_iota():
    sub = lax.broadcasted_iota(jnp.int32, (8, LANES), 0)
    lane = lax.broadcasted_iota(jnp.int32, (8, LANES), 1)
    return sub, lane


def swap_parts(tile):
    return jnp.concatenate([tile[4:8], tile[0:4]], axis=0)


def sin_cos(angle):
    quarter = jnp.floor(angle * (2.0 / jnp.pi) + 0.5)
    rest = angle - quarter * 1.5703125
    rest = rest - quarter * 4.837512969970703125e-4
    rest = rest - quarter * 7.54978995489188e-8
    square = rest * rest
    sine = -1.9515295891e-4 * square + 8.3321608736e-3
    sine = (sine * square - 1.6666654611e-1) * square * rest + rest
    cosine = 2.443315711809948e-5 * square - 1.388731625493765e-3
    cosine = (cosine * square + 4.166664568298827e-2) * square * square - 0.5 * square + 1.0
    number = quarter.astype(jnp.int32)
    odd = (number & 1) == 1
    first, second = jnp.where(odd, cosine, sine), jnp.where(odd, sine, cosine)
    first = jnp.where((number & 2) == 2, -first, first)
    second = jnp.where(((number + 1) & 2) == 2, -second, second)
    return first, second


def fill_phases(table, rows, first_row, total_rows, total_cols):
    sub, lane = tile_iota()
    block = sub % 4
    sample = 2 * ((block % 2) * LANES + lane) + block // 2
    azimuth = sample.astype(jnp.float32) * (2.0 * jnp.pi / total_cols)
    low = sub < 4
    sin_azimuth, cos_azimuth = sin_cos(azimuth)
    course = jnp.where(low, cos_azimuth, sin_azimuth)
    wave = 0.125 * total_rows
    padded = -(-len(rows) // 8) * 8
    number = lax.broadcasted_iota(jnp.int32, (padded, LANES), 0) + (first_row + rows[0])
    inside = (number >= 0) & (number < total_rows)
    polar = (number.astype(jnp.float32) + 0.5) * (jnp.pi / total_rows)
    sin_polar, cos_polar = sin_cos(polar)
    sin_z, cos_z = sin_cos(wave * cos_polar)
    sin_polar = wave * sin_polar
    cos_z, sin_z = jnp.where(inside, cos_z, 0.0), jnp.where(inside, sin_z, 0.0)
    for i in range(len(rows)):
        sin_a, cos_a = sin_cos(sin_polar[i : i + 1] * course)
        cos_b, sin_b = swap_parts(cos_a), swap_parts(sin_a)
        cx, cy = jnp.where(low, cos_a, cos_b), jnp.where(low, cos_b, cos_a)
        sx, sy = jnp.where(low, sin_a, sin_b), jnp.where(low, sin_b, sin_a)
        cc, ss, sc, cs = cx * cy, sx * sy, sx * cy, cx * sy
        plus_c, plus_s = cc - ss, sc + cs
        minus_c, minus_s = cc + ss, sc - cs
        cz, sz = cos_z[i : i + 1], sin_z[i : i + 1]
        for p in range(4):
            x_up, y_up = p % 2 == 1, p // 2 == 1
            base_c, base_s = (plus_c, plus_s) if x_up == y_up else (minus_c, minus_s)
            if not x_up:
                base_s = -base_s
            at = (i * 4 + p) * 16
            table[at : at + 8, :] = base_c * cz - base_s * sz
            table[at + 8 : at + 16, :] = base_s * cz + base_c * sz


def azimuth_weights(cols, transpose):
    i = lax.broadcasted_iota(jnp.int32, (cols, cols), 0)
    j = lax.broadcasted_iota(jnp.int32, (cols, cols), 1)
    shift = (j - i if transpose else i - j) % cols
    near = (shift == 0) | (shift == 1)
    far = (shift == cols - 1) | (shift == 2)
    return jnp.where(near, 0.5625, jnp.where(far, -0.0625, 0.0)).astype(jnp.bfloat16)


def split_dot(values, weights):
    high = values.astype(jnp.bfloat16)
    rest = (values - high.astype(jnp.float32)).astype(jnp.bfloat16)
    both = jnp.concatenate([high, rest], axis=0)
    out = jnp.dot(both, weights, preferred_element_type=jnp.float32)
    count = values.shape[0]
    return out[:count] + out[count:]


def weighted(terms):
    total = None
    for coef, tile in terms:
        part = coef * tile
        total = part if total is None else total + part
    return total


def aggregate(x_ref, tiles, table, rows, store):
    boxes = x_ref.shape[1] // 64
    weights = azimuth_weights(x_ref.shape[2], False)
    sub, _ = tile_iota()
    sign = jnp.where(sub < 4, 1.0, -1.0).astype(jnp.float32)

    def refine(b):
        parts = []
        for part in range(2):
            kids = [x_ref[part, pl.ds(pl.multiple_of(b * 64 + c * 8, 8), 8), :] for c in range(KIDS)]
            both = [kids[4 + p] + kids[3 - p] for p in range(4)]
            both += [kids[4 + p] - kids[3 - p] for p in range(4)]
            parts.append(jnp.concatenate(both, axis=0))
        even = jnp.concatenate(parts, axis=0)
        odd = split_dot(even, weights)
        for part in range(2):
            for block in range(4):
                source = even if block < 2 else odd
                lanes = slice((block % 2) * LANES, (block % 2 + 1) * LANES)
                tiles[pl.ds(b * 512 + part * 4 + block, 64, stride=8), :] = source[
                    part * 64 : part * 64 + 64, lanes
                ]

    def combine(b):
        for i, r in enumerate(rows):
            taps = [(TAP[r - 2 * k], k) for k in range(8) if r - 2 * k in TAP]
            total, turned = None, None
            for p in range(4):
                sums = []
                for q in (p, 4 + p):
                    parts = []
                    for coef, k in taps:
                        at = pl.multiple_of(b * 512 + (q * 8 + k) * 8, 8)
                        parts.append((coef, tiles[pl.ds(at, 8), :]))
                    sums.append(weighted(parts))
                at = (i * 4 + p) * 16
                first = sums[0] * table[at : at + 8, :]
                second = sums[1] * table[at + 8 : at + 16, :]
                total = first if total is None else total + first
                turned = second if turned is None else turned + second
            store(i, b, total + swap_parts(turned) * sign)

    def box(b, carry):
        refine(b)
        combine(b)
        return carry

    lax.fori_loop(0, boxes, box, 0, unroll=4)


def edge_kernel(sizes, x_ref, out_ref, table, same_ref, tiles):
    fill_phases(table, EDGE_ROWS, lax.axis_index("dir") * 16, *sizes)

    def store(i, b, tile):
        out_ref[pl.ds(pl.multiple_of(i * 64 + b * 8, 8), 8), :] = tile

    aggregate(x_ref, tiles, table, EDGE_ROWS, store)


def main_kernel(sizes, x_ref, lists_ref, out_ref, table, tiles):
    fill_phases(table, MAIN_ROWS, lax.axis_index("dir") * 16, *sizes)

    def store(i, b, tile):
        out_ref[pl.ds(pl.multiple_of(i * 72 + b * 8, 8), 8), :] = tile

    aggregate(x_ref, tiles, table, MAIN_ROWS, store)
    boxes, entries = lists_ref.shape[0] // 2, lists_ref.shape[1]
    source = lists_ref[:boxes, :]
    used = source >= 0
    at = jnp.where(used, (source + source // boxes) * 8, 0)
    by = jnp.where(used, lists_ref[boxes:, :], OPERATORS) * 16
    out_ref[64:72, :] = jnp.zeros((8, LANES), jnp.float32)
    out_ref[64:72, 0:entries] = at.astype(jnp.float32)
    out_ref[64:72, 32 : 32 + entries] = by.astype(jnp.float32)
    note = out_ref[64:72, :]
    for r in range(1, len(MAIN_ROWS)):
        out_ref[r * 72 + 64 : r * 72 + 72, :] = note


def join_kernel(own_ref, edge_ref, out_ref):
    count = len(EDGE_ROWS)
    for i in range(count):
        out_ref[i * 72 : i * 72 + 64, :] = (
            own_ref[i * 72 : i * 72 + 64, :] + edge_ref[i * 64 : i * 64 + 64, :]
        )
        out_ref[i * 72 + 64 : i * 72 + 72, :] = own_ref[i * 72 + 64 : i * 72 + 72, :]
    out_ref[count * 72 :, :] = own_ref[count * 72 :, :]


def pick_kernel(all_ref, out_ref, block_ref, sem):
    rows = all_ref.shape[1]
    wanted = (lax.axis_index("box") + rows - HALO) % rows
    near = pl.ds(pl.multiple_of(wanted // 8 * 8, 8), 8)
    copy = pltpu.make_async_copy(all_ref.at[:, near, :], block_ref, sem)
    copy.start()
    copy.wait()
    at = wanted % 8

    def eight(i, carry):
        first = pl.multiple_of(i * 8, 8)
        rows = [block_ref[first + n, pl.ds(at, 1), :] for n in range(8)]
        out_ref[pl.ds(first, 8), :] = jnp.concatenate(rows, axis=0)
        return carry

    lax.fori_loop(0, out_ref.shape[0] // 8, eight, 0)


def sort_kernel(row_ref, out_ref):
    count, wide = row_ref.shape
    source = lax.broadcasted_iota(jnp.int32, (wide, wide), 0)
    target = lax.broadcasted_iota(jnp.int32, (wide, wide), 1)
    half = wide // 2
    wanted = jnp.where(target < half, 2 * target, 2 * (target - half) + 1)
    pick = jnp.where(source == wanted, 1.0, 0.0).astype(jnp.bfloat16)
    values = row_ref[...]
    high = values.astype(jnp.bfloat16)
    rest = values - high.astype(jnp.float32)
    middle = rest.astype(jnp.bfloat16)
    low = (rest - middle.astype(jnp.float32)).astype(jnp.bfloat16)
    three = jnp.dot(
        jnp.concatenate([high, middle, low], axis=0), pick, preferred_element_type=jnp.float32
    )
    in_order = three[:count] + three[count : 2 * count] + three[2 * count :]
    for block in range(4):
        part = in_order[:, block * LANES : (block + 1) * LANES]
        out_ref[pl.ds(block, count, stride=8), :] = part
        out_ref[pl.ds(block + 4, count, stride=8), :] = part
    out_ref[count * 8 : count * 8 + 16, :] = jnp.zeros((16, LANES), jnp.float32)


def translate_kernel(entries, x_ref, operator_ref, out_ref, notes, scalars, sems):
    pairs = out_ref.shape[0] // 128
    sub, lane = tile_iota()
    for h in range(pairs):
        at = h * 144 + 64
        first, second = x_ref[at : at + 8, :], x_ref[at + 72 : at + 80, :]
        both = jnp.where(lane < 64, first, pltpu.roll(second, 64, 1))
        notes[h * 8 : h * 8 + 8, :] = both.astype(jnp.int32)

    def copy(h):
        at = pl.ds(h * 8, 8)
        return pltpu.make_async_copy(notes.at[at, :], scalars.at[at, :], sems.at[h])

    for h in range(pairs):
        copy(h).start()
    sign = jnp.where(sub < 4, -1.0, 1.0).astype(jnp.float32)

    for h in range(pairs):
        copy(h).wait()
        for g in range(2):
            for base in (0, 4):
                sums = [[None, None] for _ in range(4)]
                for k in range(entries):
                    for j in range(4):
                        row = h * 8 + base + j
                        at = pl.multiple_of(scalars[row, g * 64 + k], 8)
                        by = pl.multiple_of(scalars[row, g * 64 + 32 + k], 8)
                        pattern = x_ref[pl.ds(at, 8), :]
                        for which in range(2):
                            part = pattern * operator_ref[pl.ds(by + 8 * which, 8), :]
                            total = sums[j][which]
                            sums[j][which] = part if total is None else total + part
                for j in range(4):
                    at = h * 128 + g * 64 + (base + j) * 8
                    out_ref[at : at + 8, :] = sums[j][0] + swap_parts(sums[j][1]) * sign


def shift_sums(b, get_row, table, rows, kids, sign, put):
    plain = [get_row(i, b) for i in range(len(rows))]
    turned = [swap_parts(tile) * sign for tile in plain]
    for p in range(4):
        sums = []
        for which, source in enumerate((plain, turned)):
            product = []
            for i in range(len(rows)):
                at = (i * 4 + p) * 16 + which * 8
                product.append(source[i] * table[at : at + 8, :])
            per_row = []
            for k in kids:
                terms = [(TAP[r - 2 * k], product[i]) for i, r in enumerate(rows) if r - 2 * k in TAP]
                per_row.append(weighted(terms))
            sums.append(per_row)
        for n, k in enumerate(kids):
            put(4 + p, k, sums[0][n] + sums[1][n])
            put(3 - p, k, sums[0][n] - sums[1][n])


def turn_sign():
    sub, _ = tile_iota()
    return jnp.where(sub < 4, -1.0, 1.0).astype(jnp.float32)


def azimuth_back(tiles, base, rows, weights):
    even, odd = [], []
    for part in range(2):
        blocks = [tiles[pl.ds(base + part * 4 + block, rows, stride=8), :] for block in range(4)]
        even.append(jnp.concatenate(blocks[:2], axis=1))
        odd.append(jnp.concatenate(blocks[2:], axis=1))
    mixed = split_dot(jnp.concatenate(odd, axis=0), weights)
    return [even[part] + mixed[part * rows : part * rows + rows] for part in range(2)]


def inner_kernel(r_ref, table, out_ref, tiles):
    boxes, cols = out_ref.shape[1] // 64, out_ref.shape[2]
    weights = azimuth_weights(cols, True)
    sign = turn_sign()

    def get_row(i, b):
        return r_ref[pl.ds(pl.multiple_of(i * 64 + b * 8, 8), 8), :]

    def shift(b, carry):
        def put(c, k, tile):
            tiles[pl.ds(pl.multiple_of(b * 512 + (c * 8 + k) * 8, 8), 8), :] = tile

        shift_sums(b, get_row, table, MAIN_ROWS, tuple(range(8)), sign, put)
        values = azimuth_back(tiles, b * 512, 64, weights)
        for part in range(2):
            out_ref[part, pl.ds(pl.multiple_of(b * 64, 64), 64), :] = values[part]
        return carry

    lax.fori_loop(0, boxes, shift, 0, unroll=2)


def outer_kernel(edge_ref, table, part_ref, out_hbm, out_ref, tiles, sems):
    boxes, cols = out_ref.shape[1] // 64, out_ref.shape[2]
    weights = azimuth_weights(cols, True)
    sign = turn_sign()
    nothing = jnp.zeros((8, LANES), jnp.float32)

    def get_row(i, b):
        return edge_ref[pl.ds(pl.multiple_of(i * 64 + b * 8, 8), 8), :]

    def copy(part, b):
        at = pl.ds(pl.multiple_of(b * 64, 64), 64)
        return pltpu.make_async_copy(
            out_ref.at[part, at, :], out_hbm.at[part, at, :], sems.at[part, b]
        )

    blank = jnp.zeros((4, cols), jnp.float32)

    def box(b, carry):
        def put(c, k, tile):
            tiles[pl.ds(pl.multiple_of(b * 256 + (c * 4 + k - 4) * 8, 8), 8), :] = tile

        for c in range(KIDS):
            put(c, 4, nothing)
        shift_sums(b, get_row, table, EDGE_ROWS, (5, 6, 7), sign, put)
        values = azimuth_back(tiles, b * 256, 32, weights)
        at = pl.ds(pl.multiple_of(b * 64, 64), 64)
        for part in range(2):
            pieces = []
            for c in range(KIDS):
                pieces += [blank, values[part][c * 4 : c * 4 + 4]]
            out_ref[part, at, :] = part_ref[part, at, :] + jnp.concatenate(pieces, axis=0)
            copy(part, b).start()
        return carry

    lax.fori_loop(0, boxes, box, 0, unroll=4)
    for b in range(boxes):
        for part in range(2):
            copy(part, b).wait()


def to_next(value, step):
    size = lax.axis_size("dir")
    return lax.ppermute(value, "dir", [(i, (i + step) % size) for i in range(size)])


def call(kernel, outs, scratch, flops, moved, *args, in_hbm=(), out_hbm=False, limit=VMEM, aliases=None):
    whole = pl.BlockSpec(memory_space=pltpu.VMEM)
    far = pl.BlockSpec(memory_space=pltpu.HBM)
    out_specs = [whole] * len(outs) if isinstance(outs, list) else far if out_hbm else whole
    return pl.pallas_call(
        kernel,
        out_shape=outs,
        in_specs=[far if i in in_hbm else whole for i in range(len(args))],
        out_specs=out_specs,
        scratch_shapes=scratch,
        input_output_aliases=aliases or {},
        compiler_params=pltpu.CompilerParams(vmem_limit_bytes=limit),
        cost_estimate=pl.CostEstimate(flops=flops, bytes_accessed=moved, transcendentals=0),
    )(*args)


def on_device(child_patterns, translation, source_list, operator_list):
    parts, boxes, kids, half_rows, cols = child_patterns.shape
    local_rows = 2 * half_rows
    sizes = (local_rows * lax.axis_size("dir"), 2 * cols)
    groups = lax.axis_size("box")
    operators = translation.shape[0]
    f32 = jnp.float32
    shape = jax.ShapeDtypeStruct
    x = child_patterns.reshape(parts, boxes * kids * half_rows, cols)
    work = pltpu.VMEM((boxes * 512, LANES), f32)
    sems = pltpu.SemaphoreType.DMA((parts, boxes))
    edge = len(EDGE_ROWS)

    share, edge_table, x = call(
        functools.partial(edge_kernel, sizes),
        [
            shape((edge * boxes * 8, LANES), f32),
            shape((edge * 64, LANES), f32),
            shape(x.shape, f32),
        ],
        [work],
        10**7,
        10**6,
        x,
        aliases={0: 2},
    )
    share, source_list, operator_list = lax.optimization_barrier(
        (share, source_list, operator_list)
    )
    from_last = to_next(share, 1)
    own, main_table = call(
        functools.partial(main_kernel, sizes),
        [shape((local_rows * 72, LANES), f32), shape((local_rows * 64, LANES), f32)],
        [work],
        2 * 10**7,
        4 * 10**6,
        x,
        jnp.concatenate([source_list, operator_list]),
    )
    parent = call(join_kernel, shape(own.shape, f32), [], 10**5, 10**6, own, from_last)

    parent, translation = lax.optimization_barrier((parent, translation))
    place = lax.axis_index("box")
    row = call(
        pick_kernel,
        shape((operators * 2, 2 * cols), f32),
        [pltpu.VMEM((operators * 2, 8, 2 * cols), f32), pltpu.SemaphoreType.DMA],
        2 * 10**7,
        4 * 10**6,
        translation.reshape(operators * 2, local_rows, 2 * cols),
        in_hbm=(0,),
        limit=PICK_VMEM,
    )
    row = jnp.where(place < HALO, to_next(row, 1), row)
    sorted_operators = call(
        sort_kernel, shape(((operators + 1) * 16, LANES), f32), [], 2 * 10**7, 4 * 10**6, row
    )
    patterns = lax.all_to_all(
        parent.reshape(local_rows, 72, LANES), "box", 0, 0, tiled=True
    ).reshape(groups * 72, LANES)
    received = call(
        functools.partial(translate_kernel, source_list.shape[1]),
        shape((groups * 64, LANES), f32),
        [
            pltpu.VMEM((groups * 4, LANES), jnp.int32),
            pltpu.SMEM((groups * 4, LANES), jnp.int32),
            pltpu.SemaphoreType.DMA((groups // 2,)),
        ],
        2 * 10**7,
        2 * 10**6,
        patterns,
        sorted_operators,
    )
    received = received.reshape(groups, 64, LANES)
    received = lax.all_to_all(received, "box", 0, 0, tiled=True)
    received = received.reshape(local_rows * 64, LANES)
    from_next = to_next(received[: edge * 64], -1)
    inner = call(
        inner_kernel, shape(x.shape, f32), [work], 2 * 10**7, 4 * 10**6, received, main_table
    )
    out = call(
        outer_kernel,
        shape(x.shape, f32),
        [pltpu.VMEM(x.shape, f32), pltpu.VMEM((boxes * 256, LANES), f32), sems],
        10**7,
        2 * 10**6,
        from_next,
        edge_table,
        inner,
        out_hbm=True,
    )
    return out.reshape(child_patterns.shape)


def solution(mesh):
    return jax.shard_map(
        on_device,
        mesh=mesh,
        in_specs=(
            P(None, "box", None, "dir", None),
            P(None, None, "dir", None),
            P("box", None),
            P("box", None),
        ),
        out_specs=P(None, "box", None, "dir", None),
        check_vma=False,
    )
```

```python
import functools

import jax
import jax.numpy as jnp
from jax import lax
from jax.experimental import pallas as pl
from jax.experimental.pallas import tpu as pltpu
from jax.sharding import PartitionSpec as P

TAP = {
    -3: -0.0390625,
    -2: -0.0546875,
    -1: 0.2734375,
    0: 0.8203125,
    1: 0.8203125,
    2: 0.2734375,
    3: -0.0546875,
    4: -0.0390625,
}
KIDS = 8
HALO = 3
LANES = 128
OPERATORS = 32
MAIN_ROWS = tuple(range(-3, 13))
EDGE_ROWS = tuple(range(13, 19))
VMEM = 24 * 1024 * 1024
PICK_VMEM = 61_500_000


def tile_iota():
    sub = lax.broadcasted_iota(jnp.int32, (8, LANES), 0)
    lane = lax.broadcasted_iota(jnp.int32, (8, LANES), 1)
    return sub, lane


def swap_parts(tile):
    return jnp.concatenate([tile[4:8], tile[0:4]], axis=0)


def sin_cos(angle):
    quarter = jnp.floor(angle * (2.0 / jnp.pi) + 0.5)
    rest = angle - quarter * 1.5703125
    rest = rest - quarter * 4.837512969970703125e-4
    rest = rest - quarter * 7.54978995489188e-8
    square = rest * rest
    sine = -1.9515295891e-4 * square + 8.3321608736e-3
    sine = (sine * square - 1.6666654611e-1) * square * rest + rest
    cosine = 2.443315711809948e-5 * square - 1.388731625493765e-3
    cosine = (cosine * square + 4.166664568298827e-2) * square * square - 0.5 * square + 1.0
    number = quarter.astype(jnp.int32)
    odd = (number & 1) == 1
    first, second = jnp.where(odd, cosine, sine), jnp.where(odd, sine, cosine)
    first = jnp.where((number & 2) == 2, -first, first)
    second = jnp.where(((number + 1) & 2) == 2, -second, second)
    return first, second


def fill_phases(table, rows, first_row, total_rows, total_cols):
    sub, lane = tile_iota()
    block = sub % 4
    sample = 2 * ((block % 2) * LANES + lane) + block // 2
    azimuth = sample.astype(jnp.float32) * (2.0 * jnp.pi / total_cols)
    low = sub < 4
    sin_azimuth, cos_azimuth = sin_cos(azimuth)
    course = jnp.where(low, cos_azimuth, sin_azimuth)
    wave = 0.125 * total_rows
    padded = -(-len(rows) // 8) * 8
    number = lax.broadcasted_iota(jnp.int32, (padded, LANES), 0) + (first_row + rows[0])
    inside = (number >= 0) & (number < total_rows)
    polar = (number.astype(jnp.float32) + 0.5) * (jnp.pi / total_rows)
    sin_polar, cos_polar = sin_cos(polar)
    sin_z, cos_z = sin_cos(wave * cos_polar)
    sin_polar = wave * sin_polar
    cos_z, sin_z = jnp.where(inside, cos_z, 0.0), jnp.where(inside, sin_z, 0.0)
    for i in range(len(rows)):
        sin_a, cos_a = sin_cos(sin_polar[i : i + 1] * course)
        cos_b, sin_b = swap_parts(cos_a), swap_parts(sin_a)
        cx, cy = jnp.where(low, cos_a, cos_b), jnp.where(low, cos_b, cos_a)
        sx, sy = jnp.where(low, sin_a, sin_b), jnp.where(low, sin_b, sin_a)
        cc, ss, sc, cs = cx * cy, sx * sy, sx * cy, cx * sy
        plus_c, plus_s = cc - ss, sc + cs
        minus_c, minus_s = cc + ss, sc - cs
        cz, sz = cos_z[i : i + 1], sin_z[i : i + 1]
        for p in range(4):
            x_up, y_up = p % 2 == 1, p // 2 == 1
            base_c, base_s = (plus_c, plus_s) if x_up == y_up else (minus_c, minus_s)
            if not x_up:
                base_s = -base_s
            at = (i * 4 + p) * 16
            table[at : at + 8, :] = base_c * cz - base_s * sz
            table[at + 8 : at + 16, :] = base_s * cz + base_c * sz


def azimuth_weights(cols, transpose):
    i = lax.broadcasted_iota(jnp.int32, (cols, cols), 0)
    j = lax.broadcasted_iota(jnp.int32, (cols, cols), 1)
    shift = (j - i if transpose else i - j) % cols
    near = (shift == 0) | (shift == 1)
    far = (shift == cols - 1) | (shift == 2)
    return jnp.where(near, 0.5625, jnp.where(far, -0.0625, 0.0)).astype(jnp.bfloat16)


def split_dot(values, weights):
    high = values.astype(jnp.bfloat16)
    rest = (values - high.astype(jnp.float32)).astype(jnp.bfloat16)
    both = jnp.concatenate([high, rest], axis=0)
    out = jnp.dot(both, weights, preferred_element_type=jnp.float32)
    count = values.shape[0]
    return out[:count] + out[count:]


def weighted(terms):
    total = None
    for coef, tile in terms:
        part = coef * tile
        total = part if total is None else total + part
    return total


def aggregate(x_ref, tiles, table, rows, store):
    boxes = x_ref.shape[1] // 64
    weights = azimuth_weights(x_ref.shape[2], False)
    sub, _ = tile_iota()
    sign = jnp.where(sub < 4, 1.0, -1.0).astype(jnp.float32)

    def refine(b):
        parts = []
        for part in range(2):
            kids = [x_ref[part, pl.ds(pl.multiple_of(b * 64 + c * 8, 8), 8), :] for c in range(KIDS)]
            both = [kids[4 + p] + kids[3 - p] for p in range(4)]
            both += [kids[4 + p] - kids[3 - p] for p in range(4)]
            parts.append(jnp.concatenate(both, axis=0))
        even = jnp.concatenate(parts, axis=0)
        odd = split_dot(even, weights)
        for part in range(2):
            for block in range(4):
                source = even if block < 2 else odd
                lanes = slice((block % 2) * LANES, (block % 2 + 1) * LANES)
                tiles[pl.ds(b * 512 + part * 4 + block, 64, stride=8), :] = source[
                    part * 64 : part * 64 + 64, lanes
                ]

    def combine(b):
        for i, r in enumerate(rows):
            taps = [(TAP[r - 2 * k], k) for k in range(8) if r - 2 * k in TAP]
            total, turned = None, None
            for p in range(4):
                sums = []
                for q in (p, 4 + p):
                    parts = []
                    for coef, k in taps:
                        at = pl.multiple_of(b * 512 + (q * 8 + k) * 8, 8)
                        parts.append((coef, tiles[pl.ds(at, 8), :]))
                    sums.append(weighted(parts))
                at = (i * 4 + p) * 16
                first = sums[0] * table[at : at + 8, :]
                second = sums[1] * table[at + 8 : at + 16, :]
                total = first if total is None else total + first
                turned = second if turned is None else turned + second
            store(i, b, total + swap_parts(turned) * sign)

    def box(b, carry):
        refine(b)
        combine(b)
        return carry

    lax.fori_loop(0, boxes, box, 0, unroll=8)


def edge_kernel(sizes, x_ref, out_ref, table, same_ref, tiles):
    fill_phases(table, EDGE_ROWS, lax.axis_index("dir") * 16, *sizes)

    def store(i, b, tile):
        out_ref[pl.ds(pl.multiple_of(i * 64 + b * 8, 8), 8), :] = tile

    aggregate(x_ref, tiles, table, EDGE_ROWS, store)


def main_kernel(sizes, x_ref, lists_ref, out_ref, table, tiles):
    fill_phases(table, MAIN_ROWS, lax.axis_index("dir") * 16, *sizes)

    def store(i, b, tile):
        out_ref[pl.ds(pl.multiple_of(i * 72 + b * 8, 8), 8), :] = tile

    aggregate(x_ref, tiles, table, MAIN_ROWS, store)
    boxes, entries = lists_ref.shape[0] // 2, lists_ref.shape[1]
    source = lists_ref[:boxes, :]
    used = source >= 0
    at = jnp.where(used, (source + source // boxes) * 8, 0)
    by = jnp.where(used, lists_ref[boxes:, :], OPERATORS) * 16
    out_ref[64:72, :] = jnp.zeros((8, LANES), jnp.float32)
    out_ref[64:72, 0:entries] = at.astype(jnp.float32)
    out_ref[64:72, 32 : 32 + entries] = by.astype(jnp.float32)
    note = out_ref[64:72, :]
    for r in range(1, len(MAIN_ROWS)):
        out_ref[r * 72 + 64 : r * 72 + 72, :] = note


def join_kernel(own_ref, edge_ref, out_ref):
    count = len(EDGE_ROWS)
    for i in range(count):
        out_ref[i * 72 : i * 72 + 64, :] = (
            own_ref[i * 72 : i * 72 + 64, :] + edge_ref[i * 64 : i * 64 + 64, :]
        )
        out_ref[i * 72 + 64 : i * 72 + 72, :] = own_ref[i * 72 + 64 : i * 72 + 72, :]
    out_ref[count * 72 :, :] = own_ref[count * 72 :, :]


def pick_kernel(all_ref, out_ref, block_ref, sem):
    rows = all_ref.shape[1]
    wanted = (lax.axis_index("box") + rows - HALO) % rows
    near = pl.ds(pl.multiple_of(wanted // 8 * 8, 8), 8)
    copy = pltpu.make_async_copy(all_ref.at[:, near, :], block_ref, sem)
    copy.start()
    copy.wait()
    at = wanted % 8

    def eight(i, carry):
        first = pl.multiple_of(i * 8, 8)
        rows = [block_ref[first + n, pl.ds(at, 1), :] for n in range(8)]
        out_ref[pl.ds(first, 8), :] = jnp.concatenate(rows, axis=0)
        return carry

    lax.fori_loop(0, out_ref.shape[0] // 8, eight, 0)


def sort_kernel(row_ref, out_ref):
    count, wide = row_ref.shape
    source = lax.broadcasted_iota(jnp.int32, (wide, wide), 0)
    target = lax.broadcasted_iota(jnp.int32, (wide, wide), 1)
    half = wide // 2
    wanted = jnp.where(target < half, 2 * target, 2 * (target - half) + 1)
    pick = jnp.where(source == wanted, 1.0, 0.0).astype(jnp.bfloat16)
    values = row_ref[...]
    high = values.astype(jnp.bfloat16)
    rest = values - high.astype(jnp.float32)
    middle = rest.astype(jnp.bfloat16)
    low = (rest - middle.astype(jnp.float32)).astype(jnp.bfloat16)
    three = jnp.dot(
        jnp.concatenate([high, middle, low], axis=0), pick, preferred_element_type=jnp.float32
    )
    in_order = three[:count] + three[count : 2 * count] + three[2 * count :]
    for block in range(4):
        part = in_order[:, block * LANES : (block + 1) * LANES]
        out_ref[pl.ds(block, count, stride=8), :] = part
        out_ref[pl.ds(block + 4, count, stride=8), :] = part
    out_ref[count * 8 : count * 8 + 16, :] = jnp.zeros((16, LANES), jnp.float32)


def translate_kernel(entries, x_ref, operator_ref, out_ref, notes, scalars, sems):
    pairs = out_ref.shape[0] // 128
    sub, lane = tile_iota()
    for h in range(pairs):
        at = h * 144 + 64
        first, second = x_ref[at : at + 8, :], x_ref[at + 72 : at + 80, :]
        both = jnp.where(lane < 64, first, pltpu.roll(second, 64, 1))
        notes[h * 8 : h * 8 + 8, :] = both.astype(jnp.int32)

    def copy(h):
        at = pl.ds(h * 8, 8)
        return pltpu.make_async_copy(notes.at[at, :], scalars.at[at, :], sems.at[h])

    for h in range(pairs):
        copy(h).start()
    sign = jnp.where(sub < 4, -1.0, 1.0).astype(jnp.float32)

    for h in range(pairs):
        copy(h).wait()
        for g in range(2):
            for base in (0, 4):
                sums = [[None, None] for _ in range(4)]
                for k in range(entries):
                    for j in range(4):
                        row = h * 8 + base + j
                        at = pl.multiple_of(scalars[row, g * 64 + k], 8)
                        by = pl.multiple_of(scalars[row, g * 64 + 32 + k], 8)
                        pattern = x_ref[pl.ds(at, 8), :]
                        for which in range(2):
                            part = pattern * operator_ref[pl.ds(by + 8 * which, 8), :]
                            total = sums[j][which]
                            sums[j][which] = part if total is None else total + part
                for j in range(4):
                    at = h * 128 + g * 64 + (base + j) * 8
                    out_ref[at : at + 8, :] = sums[j][0] + swap_parts(sums[j][1]) * sign


def shift_sums(b, get_row, table, rows, kids, sign, put):
    plain = [get_row(i, b) for i in range(len(rows))]
    turned = [swap_parts(tile) * sign for tile in plain]
    for p in range(4):
        sums = []
        for which, source in enumerate((plain, turned)):
            product = []
            for i in range(len(rows)):
                at = (i * 4 + p) * 16 + which * 8
                product.append(source[i] * table[at : at + 8, :])
            per_row = []
            for k in kids:
                terms = [(TAP[r - 2 * k], product[i]) for i, r in enumerate(rows) if r - 2 * k in TAP]
                per_row.append(weighted(terms))
            sums.append(per_row)
        for n, k in enumerate(kids):
            put(4 + p, k, sums[0][n] + sums[1][n])
            put(3 - p, k, sums[0][n] - sums[1][n])


def turn_sign():
    sub, _ = tile_iota()
    return jnp.where(sub < 4, -1.0, 1.0).astype(jnp.float32)


def azimuth_back(tiles, base, rows, weights):
    even, odd = [], []
    for part in range(2):
        blocks = [tiles[pl.ds(base + part * 4 + block, rows, stride=8), :] for block in range(4)]
        even.append(jnp.concatenate(blocks[:2], axis=1))
        odd.append(jnp.concatenate(blocks[2:], axis=1))
    mixed = split_dot(jnp.concatenate(odd, axis=0), weights)
    return [even[part] + mixed[part * rows : part * rows + rows] for part in range(2)]


def inner_kernel(r_ref, table, out_ref, tiles):
    boxes, cols = out_ref.shape[1] // 64, out_ref.shape[2]
    weights = azimuth_weights(cols, True)
    sign = turn_sign()

    def get_row(i, b):
        return r_ref[pl.ds(pl.multiple_of(i * 64 + b * 8, 8), 8), :]

    def shift(b, carry):
        def put(c, k, tile):
            tiles[pl.ds(pl.multiple_of(b * 512 + (c * 8 + k) * 8, 8), 8), :] = tile

        shift_sums(b, get_row, table, MAIN_ROWS, tuple(range(8)), sign, put)
        values = azimuth_back(tiles, b * 512, 64, weights)
        for part in range(2):
            out_ref[part, pl.ds(pl.multiple_of(b * 64, 64), 64), :] = values[part]
        return carry

    lax.fori_loop(0, boxes, shift, 0, unroll=2)


def outer_kernel(edge_ref, table, part_ref, out_hbm, out_ref, tiles, sems):
    boxes, cols = out_ref.shape[1] // 64, out_ref.shape[2]
    weights = azimuth_weights(cols, True)
    sign = turn_sign()
    nothing = jnp.zeros((8, LANES), jnp.float32)

    def get_row(i, b):
        return edge_ref[pl.ds(pl.multiple_of(i * 64 + b * 8, 8), 8), :]

    def copy(part, b):
        at = pl.ds(pl.multiple_of(b * 64, 64), 64)
        return pltpu.make_async_copy(
            out_ref.at[part, at, :], out_hbm.at[part, at, :], sems.at[part, b]
        )

    blank = jnp.zeros((4, cols), jnp.float32)

    def box(b, carry):
        def put(c, k, tile):
            tiles[pl.ds(pl.multiple_of(b * 256 + (c * 4 + k - 4) * 8, 8), 8), :] = tile

        for c in range(KIDS):
            put(c, 4, nothing)
        shift_sums(b, get_row, table, EDGE_ROWS, (5, 6, 7), sign, put)
        values = azimuth_back(tiles, b * 256, 32, weights)
        at = pl.ds(pl.multiple_of(b * 64, 64), 64)
        for part in range(2):
            pieces = []
            for c in range(KIDS):
                pieces += [blank, values[part][c * 4 : c * 4 + 4]]
            out_ref[part, at, :] = part_ref[part, at, :] + jnp.concatenate(pieces, axis=0)
            copy(part, b).start()
        return carry

    lax.fori_loop(0, boxes, box, 0, unroll=8)
    for b in range(boxes):
        for part in range(2):
            copy(part, b).wait()


def to_next(value, step):
    size = lax.axis_size("dir")
    return lax.ppermute(value, "dir", [(i, (i + step) % size) for i in range(size)])


def call(kernel, outs, scratch, flops, moved, *args, in_hbm=(), out_hbm=False, limit=VMEM, aliases=None):
    whole = pl.BlockSpec(memory_space=pltpu.VMEM)
    far = pl.BlockSpec(memory_space=pltpu.HBM)
    out_specs = [whole] * len(outs) if isinstance(outs, list) else far if out_hbm else whole
    return pl.pallas_call(
        kernel,
        out_shape=outs,
        in_specs=[far if i in in_hbm else whole for i in range(len(args))],
        out_specs=out_specs,
        scratch_shapes=scratch,
        input_output_aliases=aliases or {},
        compiler_params=pltpu.CompilerParams(vmem_limit_bytes=limit),
        cost_estimate=pl.CostEstimate(flops=flops, bytes_accessed=moved, transcendentals=0),
    )(*args)


def on_device(child_patterns, translation, source_list, operator_list):
    parts, boxes, kids, half_rows, cols = child_patterns.shape
    local_rows = 2 * half_rows
    sizes = (local_rows * lax.axis_size("dir"), 2 * cols)
    groups = lax.axis_size("box")
    operators = translation.shape[0]
    f32 = jnp.float32
    shape = jax.ShapeDtypeStruct
    x = child_patterns.reshape(parts, boxes * kids * half_rows, cols)
    work = pltpu.VMEM((boxes * 512, LANES), f32)
    sems = pltpu.SemaphoreType.DMA((parts, boxes))
    edge = len(EDGE_ROWS)

    share, edge_table, x = call(
        functools.partial(edge_kernel, sizes),
        [
            shape((edge * boxes * 8, LANES), f32),
            shape((edge * 64, LANES), f32),
            shape(x.shape, f32),
        ],
        [work],
        10**7,
        10**6,
        x,
        aliases={0: 2},
    )
    share, source_list, operator_list = lax.optimization_barrier(
        (share, source_list, operator_list)
    )
    from_last = to_next(share, 1)
    own, main_table = call(
        functools.partial(main_kernel, sizes),
        [shape((local_rows * 72, LANES), f32), shape((local_rows * 64, LANES), f32)],
        [work],
        2 * 10**7,
        4 * 10**6,
        x,
        jnp.concatenate([source_list, operator_list]),
    )
    parent = call(join_kernel, shape(own.shape, f32), [], 10**5, 10**6, own, from_last)

    parent, translation = lax.optimization_barrier((parent, translation))
    place = lax.axis_index("box")
    row = call(
        pick_kernel,
        shape((operators * 2, 2 * cols), f32),
        [pltpu.VMEM((operators * 2, 8, 2 * cols), f32), pltpu.SemaphoreType.DMA],
        2 * 10**7,
        4 * 10**6,
        translation.reshape(operators * 2, local_rows, 2 * cols),
        in_hbm=(0,),
        limit=PICK_VMEM,
    )
    row = jnp.where(place < HALO, to_next(row, 1), row)
    sorted_operators = call(
        sort_kernel, shape(((operators + 1) * 16, LANES), f32), [], 2 * 10**7, 4 * 10**6, row
    )
    patterns = lax.all_to_all(
        parent.reshape(local_rows, 72, LANES), "box", 0, 0, tiled=True
    ).reshape(groups * 72, LANES)
    received = call(
        functools.partial(translate_kernel, source_list.shape[1]),
        shape((groups * 64, LANES), f32),
        [
            pltpu.VMEM((groups * 4, LANES), jnp.int32),
            pltpu.SMEM((groups * 4, LANES), jnp.int32),
            pltpu.SemaphoreType.DMA((groups // 2,)),
        ],
        2 * 10**7,
        2 * 10**6,
        patterns,
        sorted_operators,
    )
    received = received.reshape(groups, 64, LANES)
    received = lax.all_to_all(received, "box", 0, 0, tiled=True)
    received = received.reshape(local_rows * 64, LANES)
    from_next = to_next(received[: edge * 64], -1)
    inner = call(
        inner_kernel, shape(x.shape, f32), [work], 2 * 10**7, 4 * 10**6, received, main_table
    )
    out = call(
        outer_kernel,
        shape(x.shape, f32),
        [pltpu.VMEM(x.shape, f32), pltpu.VMEM((boxes * 256, LANES), f32), sems],
        10**7,
        2 * 10**6,
        from_next,
        edge_table,
        inner,
        out_hbm=True,
    )
    return out.reshape(child_patterns.shape)


def solution(mesh):
    return jax.shard_map(
        on_device,
        mesh=mesh,
        in_specs=(
            P(None, "box", None, "dir", None),
            P(None, None, "dir", None),
            P("box", None),
            P("box", None),
        ),
        out_specs=P(None, "box", None, "dir", None),
        check_vma=False,
    )
```

```python
import functools

import jax
import jax.numpy as jnp
from jax import lax
from jax.experimental import pallas as pl
from jax.experimental.pallas import tpu as pltpu
from jax.sharding import PartitionSpec as P

TAP = {
    -3: -0.0390625,
    -2: -0.0546875,
    -1: 0.2734375,
    0: 0.8203125,
    1: 0.8203125,
    2: 0.2734375,
    3: -0.0546875,
    4: -0.0390625,
}
KIDS = 8
HALO = 3
LANES = 128
OPERATORS = 32
MAIN_ROWS = tuple(range(-3, 13))
EDGE_ROWS = tuple(range(13, 19))
VMEM = 24 * 1024 * 1024
PICK_VMEM = 61_500_000


def tile_iota():
    sub = lax.broadcasted_iota(jnp.int32, (8, LANES), 0)
    lane = lax.broadcasted_iota(jnp.int32, (8, LANES), 1)
    return sub, lane


def swap_parts(tile):
    return jnp.concatenate([tile[4:8], tile[0:4]], axis=0)


def sin_cos(angle):
    quarter = jnp.floor(angle * (2.0 / jnp.pi) + 0.5)
    rest = angle - quarter * 1.5703125
    rest = rest - quarter * 4.837512969970703125e-4
    rest = rest - quarter * 7.54978995489188e-8
    square = rest * rest
    sine = -1.9515295891e-4 * square + 8.3321608736e-3
    sine = (sine * square - 1.6666654611e-1) * square * rest + rest
    cosine = 2.443315711809948e-5 * square - 1.388731625493765e-3
    cosine = (cosine * square + 4.166664568298827e-2) * square * square - 0.5 * square + 1.0
    number = quarter.astype(jnp.int32)
    odd = (number & 1) == 1
    first, second = jnp.where(odd, cosine, sine), jnp.where(odd, sine, cosine)
    first = jnp.where((number & 2) == 2, -first, first)
    second = jnp.where(((number + 1) & 2) == 2, -second, second)
    return first, second


def fill_phases(table, rows, first_row, total_rows, total_cols):
    sub, lane = tile_iota()
    block = sub % 4
    sample = 2 * ((block % 2) * LANES + lane) + block // 2
    azimuth = sample.astype(jnp.float32) * (2.0 * jnp.pi / total_cols)
    low = sub < 4
    sin_azimuth, cos_azimuth = sin_cos(azimuth)
    course = jnp.where(low, cos_azimuth, sin_azimuth)
    wave = 0.125 * total_rows
    padded = -(-len(rows) // 8) * 8
    number = lax.broadcasted_iota(jnp.int32, (padded, LANES), 0) + (first_row + rows[0])
    inside = (number >= 0) & (number < total_rows)
    polar = (number.astype(jnp.float32) + 0.5) * (jnp.pi / total_rows)
    sin_polar, cos_polar = sin_cos(polar)
    sin_z, cos_z = sin_cos(wave * cos_polar)
    sin_polar = wave * sin_polar
    cos_z, sin_z = jnp.where(inside, cos_z, 0.0), jnp.where(inside, sin_z, 0.0)
    for i in range(len(rows)):
        sin_a, cos_a = sin_cos(sin_polar[i : i + 1] * course)
        cos_b, sin_b = swap_parts(cos_a), swap_parts(sin_a)
        cx, cy = jnp.where(low, cos_a, cos_b), jnp.where(low, cos_b, cos_a)
        sx, sy = jnp.where(low, sin_a, sin_b), jnp.where(low, sin_b, sin_a)
        cc, ss, sc, cs = cx * cy, sx * sy, sx * cy, cx * sy
        plus_c, plus_s = cc - ss, sc + cs
        minus_c, minus_s = cc + ss, sc - cs
        cz, sz = cos_z[i : i + 1], sin_z[i : i + 1]
        for p in range(4):
            x_up, y_up = p % 2 == 1, p // 2 == 1
            base_c, base_s = (plus_c, plus_s) if x_up == y_up else (minus_c, minus_s)
            if not x_up:
                base_s = -base_s
            at = (i * 4 + p) * 16
            table[at : at + 8, :] = base_c * cz - base_s * sz
            table[at + 8 : at + 16, :] = base_s * cz + base_c * sz


def azimuth_weights(cols, transpose):
    i = lax.broadcasted_iota(jnp.int32, (cols, cols), 0)
    j = lax.broadcasted_iota(jnp.int32, (cols, cols), 1)
    shift = (j - i if transpose else i - j) % cols
    near = (shift == 0) | (shift == 1)
    far = (shift == cols - 1) | (shift == 2)
    return jnp.where(near, 0.5625, jnp.where(far, -0.0625, 0.0)).astype(jnp.bfloat16)


def split_dot(values, weights):
    high = values.astype(jnp.bfloat16)
    rest = (values - high.astype(jnp.float32)).astype(jnp.bfloat16)
    both = jnp.concatenate([high, rest], axis=0)
    out = jnp.dot(both, weights, preferred_element_type=jnp.float32)
    count = values.shape[0]
    return out[:count] + out[count:]


def weighted(terms):
    total = None
    for coef, tile in terms:
        part = coef * tile
        total = part if total is None else total + part
    return total


def aggregate(x_ref, tiles, table, rows, store):
    boxes = x_ref.shape[1] // 64
    weights = azimuth_weights(x_ref.shape[2], False)
    sub, _ = tile_iota()
    sign = jnp.where(sub < 4, 1.0, -1.0).astype(jnp.float32)

    def refine(b):
        parts = []
        for part in range(2):
            kids = [x_ref[part, pl.ds(pl.multiple_of(b * 64 + c * 8, 8), 8), :] for c in range(KIDS)]
            both = [kids[4 + p] + kids[3 - p] for p in range(4)]
            both += [kids[4 + p] - kids[3 - p] for p in range(4)]
            parts.append(jnp.concatenate(both, axis=0))
        even = jnp.concatenate(parts, axis=0)
        odd = split_dot(even, weights)
        for part in range(2):
            for block in range(4):
                source = even if block < 2 else odd
                lanes = slice((block % 2) * LANES, (block % 2 + 1) * LANES)
                tiles[pl.ds(b * 512 + part * 4 + block, 64, stride=8), :] = source[
                    part * 64 : part * 64 + 64, lanes
                ]

    def combine(b):
        for i, r in enumerate(rows):
            taps = [(TAP[r - 2 * k], k) for k in range(8) if r - 2 * k in TAP]
            total, turned = None, None
            for p in range(4):
                sums = []
                for q in (p, 4 + p):
                    parts = []
                    for coef, k in taps:
                        at = pl.multiple_of(b * 512 + (q * 8 + k) * 8, 8)
                        parts.append((coef, tiles[pl.ds(at, 8), :]))
                    sums.append(weighted(parts))
                at = (i * 4 + p) * 16
                first = sums[0] * table[at : at + 8, :]
                second = sums[1] * table[at + 8 : at + 16, :]
                total = first if total is None else total + first
                turned = second if turned is None else turned + second
            store(i, b, total + swap_parts(turned) * sign)

    def box(b, carry):
        refine(b)
        combine(b)
        return carry

    lax.fori_loop(0, boxes, box, 0, unroll=8)


def edge_kernel(sizes, x_ref, out_ref, table, same_ref, tiles):
    fill_phases(table, EDGE_ROWS, lax.axis_index("dir") * 16, *sizes)

    def store(i, b, tile):
        out_ref[pl.ds(pl.multiple_of(i * 64 + b * 8, 8), 8), :] = tile

    aggregate(x_ref, tiles, table, EDGE_ROWS, store)


def main_kernel(sizes, x_ref, lists_ref, out_ref, table, tiles):
    fill_phases(table, MAIN_ROWS, lax.axis_index("dir") * 16, *sizes)

    def store(i, b, tile):
        out_ref[pl.ds(pl.multiple_of(i * 72 + b * 8, 8), 8), :] = tile

    aggregate(x_ref, tiles, table, MAIN_ROWS, store)
    boxes, entries = lists_ref.shape[0] // 2, lists_ref.shape[1]
    source = lists_ref[:boxes, :]
    used = source >= 0
    at = jnp.where(used, (source + source // boxes) * 8, 0)
    by = jnp.where(used, lists_ref[boxes:, :], OPERATORS) * 16
    out_ref[64:72, :] = jnp.zeros((8, LANES), jnp.float32)
    out_ref[64:72, 0:entries] = at.astype(jnp.float32)
    out_ref[64:72, 32 : 32 + entries] = by.astype(jnp.float32)
    note = out_ref[64:72, :]
    for r in range(1, len(MAIN_ROWS)):
        out_ref[r * 72 + 64 : r * 72 + 72, :] = note


def join_kernel(own_ref, edge_ref, out_ref):
    count = len(EDGE_ROWS)
    for i in range(count):
        out_ref[i * 72 : i * 72 + 64, :] = (
            own_ref[i * 72 : i * 72 + 64, :] + edge_ref[i * 64 : i * 64 + 64, :]
        )
        out_ref[i * 72 + 64 : i * 72 + 72, :] = own_ref[i * 72 + 64 : i * 72 + 72, :]
    out_ref[count * 72 :, :] = own_ref[count * 72 :, :]


def pick_kernel(all_ref, out_ref, block_ref, sem):
    rows = all_ref.shape[1]
    wanted = (lax.axis_index("box") + rows - HALO) % rows
    near = pl.ds(pl.multiple_of(wanted // 8 * 8, 8), 8)
    copy = pltpu.make_async_copy(all_ref.at[:, near, :], block_ref, sem)
    copy.start()
    copy.wait()
    at = wanted % 8

    def eight(i, carry):
        first = pl.multiple_of(i * 8, 8)
        rows = [block_ref[first + n, pl.ds(at, 1), :] for n in range(8)]
        out_ref[pl.ds(first, 8), :] = jnp.concatenate(rows, axis=0)
        return carry

    lax.fori_loop(0, out_ref.shape[0] // 8, eight, 0)


def sort_kernel(row_ref, out_ref):
    count, wide = row_ref.shape
    source = lax.broadcasted_iota(jnp.int32, (wide, wide), 0)
    target = lax.broadcasted_iota(jnp.int32, (wide, wide), 1)
    half = wide // 2
    wanted = jnp.where(target < half, 2 * target, 2 * (target - half) + 1)
    pick = jnp.where(source == wanted, 1.0, 0.0).astype(jnp.bfloat16)
    values = row_ref[...]
    high = values.astype(jnp.bfloat16)
    rest = values - high.astype(jnp.float32)
    middle = rest.astype(jnp.bfloat16)
    low = (rest - middle.astype(jnp.float32)).astype(jnp.bfloat16)
    three = jnp.dot(
        jnp.concatenate([high, middle, low], axis=0), pick, preferred_element_type=jnp.float32
    )
    in_order = three[:count] + three[count : 2 * count] + three[2 * count :]
    for block in range(4):
        part = in_order[:, block * LANES : (block + 1) * LANES]
        out_ref[pl.ds(block, count, stride=8), :] = part
        out_ref[pl.ds(block + 4, count, stride=8), :] = part
    out_ref[count * 8 : count * 8 + 16, :] = jnp.zeros((16, LANES), jnp.float32)


def translate_kernel(entries, x_ref, operator_ref, out_ref, notes, scalars, sems):
    pairs = out_ref.shape[0] // 128
    sub, lane = tile_iota()
    for h in range(pairs):
        at = h * 144 + 64
        first, second = x_ref[at : at + 8, :], x_ref[at + 72 : at + 80, :]
        both = jnp.where(lane < 64, first, pltpu.roll(second, 64, 1))
        notes[h * 8 : h * 8 + 8, :] = both.astype(jnp.int32)

    def copy(h):
        at = pl.ds(h * 8, 8)
        return pltpu.make_async_copy(notes.at[at, :], scalars.at[at, :], sems.at[h])

    for h in range(pairs):
        copy(h).start()
    sign = jnp.where(sub < 4, -1.0, 1.0).astype(jnp.float32)

    for h in range(pairs):
        copy(h).wait()
        for g in range(2):
            for base in (0, 4):
                sums = [[None, None] for _ in range(4)]
                for k in range(entries):
                    for j in range(4):
                        row = h * 8 + base + j
                        at = pl.multiple_of(scalars[row, g * 64 + k], 8)
                        by = pl.multiple_of(scalars[row, g * 64 + 32 + k], 8)
                        pattern = x_ref[pl.ds(at, 8), :]
                        for which in range(2):
                            part = pattern * operator_ref[pl.ds(by + 8 * which, 8), :]
                            total = sums[j][which]
                            sums[j][which] = part if total is None else total + part
                for j in range(4):
                    at = h * 128 + g * 64 + (base + j) * 8
                    out_ref[at : at + 8, :] = sums[j][0] + swap_parts(sums[j][1]) * sign


def shift_sums(b, get_row, table, rows, kids, sign, put):
    plain = [get_row(i, b) for i in range(len(rows))]
    turned = [swap_parts(tile) * sign for tile in plain]
    for p in range(4):
        sums = []
        for which, source in enumerate((plain, turned)):
            product = []
            for i in range(len(rows)):
                at = (i * 4 + p) * 16 + which * 8
                product.append(source[i] * table[at : at + 8, :])
            per_row = []
            for k in kids:
                terms = [(TAP[r - 2 * k], product[i]) for i, r in enumerate(rows) if r - 2 * k in TAP]
                per_row.append(weighted(terms))
            sums.append(per_row)
        for n, k in enumerate(kids):
            put(4 + p, k, sums[0][n] + sums[1][n])
            put(3 - p, k, sums[0][n] - sums[1][n])


def turn_sign():
    sub, _ = tile_iota()
    return jnp.where(sub < 4, -1.0, 1.0).astype(jnp.float32)


def azimuth_back(tiles, base, rows, weights):
    even, odd = [], []
    for part in range(2):
        blocks = [tiles[pl.ds(base + part * 4 + block, rows, stride=8), :] for block in range(4)]
        even.append(jnp.concatenate(blocks[:2], axis=1))
        odd.append(jnp.concatenate(blocks[2:], axis=1))
    mixed = split_dot(jnp.concatenate(odd, axis=0), weights)
    return [even[part] + mixed[part * rows : part * rows + rows] for part in range(2)]


def inner_kernel(r_ref, table, out_ref, tiles):
    boxes, cols = out_ref.shape[1] // 64, out_ref.shape[2]
    weights = azimuth_weights(cols, True)
    sign = turn_sign()

    def get_row(i, b):
        return r_ref[pl.ds(pl.multiple_of(i * 64 + b * 8, 8), 8), :]

    def shift(b, carry):
        def put(c, k, tile):
            tiles[pl.ds(pl.multiple_of(b * 512 + (c * 8 + k) * 8, 8), 8), :] = tile

        shift_sums(b, get_row, table, MAIN_ROWS, tuple(range(8)), sign, put)
        values = azimuth_back(tiles, b * 512, 64, weights)
        for part in range(2):
            out_ref[part, pl.ds(pl.multiple_of(b * 64, 64), 64), :] = values[part]
        return carry

    lax.fori_loop(0, boxes, shift, 0, unroll=2)


def outer_kernel(edge_ref, table, part_ref, out_hbm, out_ref, tiles, sems):
    boxes, cols = out_ref.shape[1] // 64, out_ref.shape[2]
    weights = azimuth_weights(cols, True)
    sign = turn_sign()
    nothing = jnp.zeros((8, LANES), jnp.float32)

    def get_row(i, b):
        return edge_ref[pl.ds(pl.multiple_of(i * 64 + b * 8, 8), 8), :]

    def copy(part, b):
        at = pl.ds(pl.multiple_of(b * 64, 64), 64)
        return pltpu.make_async_copy(
            out_ref.at[part, at, :], out_hbm.at[part, at, :], sems.at[part, b]
        )

    blank = jnp.zeros((4, cols), jnp.float32)

    def box(b, carry):
        def put(c, k, tile):
            tiles[pl.ds(pl.multiple_of(b * 256 + (c * 4 + k - 4) * 8, 8), 8), :] = tile

        for c in range(KIDS):
            put(c, 4, nothing)
        shift_sums(b, get_row, table, EDGE_ROWS, (5, 6, 7), sign, put)
        values = azimuth_back(tiles, b * 256, 32, weights)
        at = pl.ds(pl.multiple_of(b * 64, 64), 64)
        for part in range(2):
            pieces = []
            for c in range(KIDS):
                pieces += [blank, values[part][c * 4 : c * 4 + 4]]
            out_ref[part, at, :] = part_ref[part, at, :] + jnp.concatenate(pieces, axis=0)
            copy(part, b).start()
        return carry

    lax.fori_loop(0, boxes, box, 0, unroll=8)
    for b in range(boxes):
        for part in range(2):
            copy(part, b).wait()


def to_next(value, step):
    size = lax.axis_size("dir")
    return lax.ppermute(value, "dir", [(i, (i + step) % size) for i in range(size)])


def call(kernel, outs, scratch, flops, moved, *args, in_hbm=(), out_hbm=False, limit=VMEM, aliases=None):
    whole = pl.BlockSpec(memory_space=pltpu.VMEM)
    far = pl.BlockSpec(memory_space=pltpu.HBM)
    out_specs = [whole] * len(outs) if isinstance(outs, list) else far if out_hbm else whole
    return pl.pallas_call(
        kernel,
        out_shape=outs,
        in_specs=[far if i in in_hbm else whole for i in range(len(args))],
        out_specs=out_specs,
        scratch_shapes=scratch,
        input_output_aliases=aliases or {},
        compiler_params=pltpu.CompilerParams(vmem_limit_bytes=limit),
        cost_estimate=pl.CostEstimate(flops=flops, bytes_accessed=moved, transcendentals=0),
    )(*args)


def on_device(child_patterns, translation, source_list, operator_list):
    parts, boxes, kids, half_rows, cols = child_patterns.shape
    local_rows = 2 * half_rows
    sizes = (local_rows * lax.axis_size("dir"), 2 * cols)
    groups = lax.axis_size("box")
    operators = translation.shape[0]
    f32 = jnp.float32
    shape = jax.ShapeDtypeStruct
    x = child_patterns.reshape(parts, boxes * kids * half_rows, cols)
    work = pltpu.VMEM((boxes * 512 + 8, LANES), f32)
    sems = pltpu.SemaphoreType.DMA((parts, boxes))
    edge = len(EDGE_ROWS)

    share, edge_table, x = call(
        functools.partial(edge_kernel, sizes),
        [
            shape((edge * boxes * 8, LANES), f32),
            shape((edge * 64, LANES), f32),
            shape(x.shape, f32),
        ],
        [work],
        10**7,
        10**6,
        x,
        aliases={0: 2},
    )
    share, source_list, operator_list = lax.optimization_barrier(
        (share, source_list, operator_list)
    )
    from_last = to_next(share, 1)
    own, main_table = call(
        functools.partial(main_kernel, sizes),
        [shape((local_rows * 72, LANES), f32), shape((local_rows * 64, LANES), f32)],
        [work],
        2 * 10**7,
        4 * 10**6,
        x,
        jnp.concatenate([source_list, operator_list]),
    )
    parent = call(join_kernel, shape(own.shape, f32), [], 10**5, 10**6, own, from_last)

    parent, translation = lax.optimization_barrier((parent, translation))
    place = lax.axis_index("box")
    row = call(
        pick_kernel,
        shape((operators * 2, 2 * cols), f32),
        [pltpu.VMEM((operators * 2, 8, 2 * cols), f32), pltpu.SemaphoreType.DMA],
        2 * 10**7,
        4 * 10**6,
        translation.reshape(operators * 2, local_rows, 2 * cols),
        in_hbm=(0,),
        limit=PICK_VMEM,
    )
    row = jnp.where(place < HALO, to_next(row, 1), row)
    sorted_operators = call(
        sort_kernel, shape(((operators + 1) * 16, LANES), f32), [], 2 * 10**7, 4 * 10**6, row
    )
    patterns = lax.all_to_all(
        parent.reshape(local_rows, 72, LANES), "box", 0, 0, tiled=True
    ).reshape(groups * 72, LANES)
    received = call(
        functools.partial(translate_kernel, source_list.shape[1]),
        shape((groups * 64, LANES), f32),
        [
            pltpu.VMEM((groups * 4, LANES), jnp.int32),
            pltpu.SMEM((groups * 4, LANES), jnp.int32),
            pltpu.SemaphoreType.DMA((groups // 2,)),
        ],
        2 * 10**7,
        2 * 10**6,
        patterns,
        sorted_operators,
    )
    received = received.reshape(groups, 64, LANES)
    received = lax.all_to_all(received, "box", 0, 0, tiled=True)
    received = received.reshape(local_rows * 64, LANES)
    from_next = to_next(received[: edge * 64], -1)
    inner = call(
        inner_kernel, shape(x.shape, f32), [work], 2 * 10**7, 4 * 10**6, received, main_table
    )
    out = call(
        outer_kernel,
        shape(x.shape, f32),
        [pltpu.VMEM(x.shape, f32), pltpu.VMEM((boxes * 256 + 8, LANES), f32), sems],
        10**7,
        2 * 10**6,
        from_next,
        edge_table,
        inner,
        out_hbm=True,
    )
    return out.reshape(child_patterns.shape)


def solution(mesh):
    return jax.shard_map(
        on_device,
        mesh=mesh,
        in_specs=(
            P(None, "box", None, "dir", None),
            P(None, None, "dir", None),
            P("box", None),
            P("box", None),
        ),
        out_specs=P(None, "box", None, "dir", None),
        check_vma=False,
    )
```

```python
import functools

import jax
import jax.numpy as jnp
from jax import lax
from jax.experimental import pallas as pl
from jax.experimental.pallas import tpu as pltpu
from jax.sharding import PartitionSpec as P

TAP = {
    -3: -0.0390625,
    -2: -0.0546875,
    -1: 0.2734375,
    0: 0.8203125,
    1: 0.8203125,
    2: 0.2734375,
    3: -0.0546875,
    4: -0.0390625,
}
KIDS = 8
HALO = 3
LANES = 128
OPERATORS = 32
MAIN_ROWS = tuple(range(-3, 13))
EDGE_ROWS = tuple(range(13, 19))
VMEM = 24 * 1024 * 1024
PICK_VMEM = 61_500_000


def tile_iota():
    sub = lax.broadcasted_iota(jnp.int32, (8, LANES), 0)
    lane = lax.broadcasted_iota(jnp.int32, (8, LANES), 1)
    return sub, lane


def swap_parts(tile):
    return jnp.concatenate([tile[4:8], tile[0:4]], axis=0)


def sin_cos(angle):
    quarter = jnp.floor(angle * (2.0 / jnp.pi) + 0.5)
    rest = angle - quarter * 1.5703125
    rest = rest - quarter * 4.837512969970703125e-4
    rest = rest - quarter * 7.54978995489188e-8
    square = rest * rest
    sine = -1.9515295891e-4 * square + 8.3321608736e-3
    sine = (sine * square - 1.6666654611e-1) * square * rest + rest
    cosine = 2.443315711809948e-5 * square - 1.388731625493765e-3
    cosine = (cosine * square + 4.166664568298827e-2) * square * square - 0.5 * square + 1.0
    number = quarter.astype(jnp.int32)
    odd = (number & 1) == 1
    first, second = jnp.where(odd, cosine, sine), jnp.where(odd, sine, cosine)
    first = jnp.where((number & 2) == 2, -first, first)
    second = jnp.where(((number + 1) & 2) == 2, -second, second)
    return first, second


def fill_phases(table, rows, first_row, total_rows, total_cols):
    sub, lane = tile_iota()
    block = sub % 4
    sample = 2 * ((block % 2) * LANES + lane) + block // 2
    azimuth = sample.astype(jnp.float32) * (2.0 * jnp.pi / total_cols)
    low = sub < 4
    sin_azimuth, cos_azimuth = sin_cos(azimuth)
    course = jnp.where(low, cos_azimuth, sin_azimuth)
    wave = 0.125 * total_rows
    padded = -(-len(rows) // 8) * 8
    number = lax.broadcasted_iota(jnp.int32, (padded, LANES), 0) + (first_row + rows[0])
    inside = (number >= 0) & (number < total_rows)
    polar = (number.astype(jnp.float32) + 0.5) * (jnp.pi / total_rows)
    sin_polar, cos_polar = sin_cos(polar)
    sin_z, cos_z = sin_cos(wave * cos_polar)
    sin_polar = wave * sin_polar
    cos_z, sin_z = jnp.where(inside, cos_z, 0.0), jnp.where(inside, sin_z, 0.0)
    for i in range(len(rows)):
        sin_a, cos_a = sin_cos(sin_polar[i : i + 1] * course)
        cos_b, sin_b = swap_parts(cos_a), swap_parts(sin_a)
        cx, cy = jnp.where(low, cos_a, cos_b), jnp.where(low, cos_b, cos_a)
        sx, sy = jnp.where(low, sin_a, sin_b), jnp.where(low, sin_b, sin_a)
        cc, ss, sc, cs = cx * cy, sx * sy, sx * cy, cx * sy
        plus_c, plus_s = cc - ss, sc + cs
        minus_c, minus_s = cc + ss, sc - cs
        cz, sz = cos_z[i : i + 1], sin_z[i : i + 1]
        for p in range(4):
            x_up, y_up = p % 2 == 1, p // 2 == 1
            base_c, base_s = (plus_c, plus_s) if x_up == y_up else (minus_c, minus_s)
            if not x_up:
                base_s = -base_s
            at = (i * 4 + p) * 16
            table[at : at + 8, :] = base_c * cz - base_s * sz
            table[at + 8 : at + 16, :] = base_s * cz + base_c * sz


def azimuth_weights(cols, transpose):
    i = lax.broadcasted_iota(jnp.int32, (cols, cols), 0)
    j = lax.broadcasted_iota(jnp.int32, (cols, cols), 1)
    shift = (j - i if transpose else i - j) & (cols - 1)
    near = (shift == 0) | (shift == 1)
    far = (shift == cols - 1) | (shift == 2)
    return jnp.where(near, 0.5625, jnp.where(far, -0.0625, 0.0)).astype(jnp.bfloat16)


def split_dot(values, weights):
    high = values.astype(jnp.bfloat16)
    rest = (values - high.astype(jnp.float32)).astype(jnp.bfloat16)
    both = jnp.concatenate([high, rest], axis=0)
    out = jnp.dot(both, weights, preferred_element_type=jnp.float32)
    count = values.shape[0]
    return out[:count] + out[count:]


def weighted(terms):
    total = None
    for coef, tile in terms:
        part = coef * tile
        total = part if total is None else total + part
    return total


def aggregate(x_ref, tiles, table, rows, store):
    boxes = x_ref.shape[1] // 64
    weights = azimuth_weights(x_ref.shape[2], False)
    sub, _ = tile_iota()
    sign = jnp.where(sub < 4, 1.0, -1.0).astype(jnp.float32)

    def refine(b):
        parts = []
        for part in range(2):
            kids = [x_ref[part, pl.ds(pl.multiple_of(b * 64 + c * 8, 8), 8), :] for c in range(KIDS)]
            both = [kids[4 + p] + kids[3 - p] for p in range(4)]
            both += [kids[4 + p] - kids[3 - p] for p in range(4)]
            parts.append(jnp.concatenate(both, axis=0))
        even = jnp.concatenate(parts, axis=0)
        odd = split_dot(even, weights)
        for part in range(2):
            for block in range(4):
                source = even if block < 2 else odd
                lanes = slice((block % 2) * LANES, (block % 2 + 1) * LANES)
                tiles[pl.ds(b * 512 + part * 4 + block, 64, stride=8), :] = source[
                    part * 64 : part * 64 + 64, lanes
                ]

    def combine(b):
        for i, r in enumerate(rows):
            taps = [(TAP[r - 2 * k], k) for k in range(8) if r - 2 * k in TAP]
            total, turned = None, None
            for p in range(4):
                sums = []
                for q in (p, 4 + p):
                    parts = []
                    for coef, k in taps:
                        at = pl.multiple_of(b * 512 + (q * 8 + k) * 8, 8)
                        parts.append((coef, tiles[pl.ds(at, 8), :]))
                    sums.append(weighted(parts))
                at = (i * 4 + p) * 16
                first = sums[0] * table[at : at + 8, :]
                second = sums[1] * table[at + 8 : at + 16, :]
                total = first if total is None else total + first
                turned = second if turned is None else turned + second
            store(i, b, total + swap_parts(turned) * sign)

    def box(b, carry):
        refine(b)
        combine(b)
        return carry

    lax.fori_loop(0, boxes, box, 0, unroll=8)


def edge_kernel(sizes, x_ref, out_ref, table, same_ref, tiles):
    fill_phases(table, EDGE_ROWS, lax.axis_index("dir") * 16, *sizes)

    def store(i, b, tile):
        out_ref[pl.ds(pl.multiple_of(i * 64 + b * 8, 8), 8), :] = tile

    aggregate(x_ref, tiles, table, EDGE_ROWS, store)


def main_kernel(sizes, x_ref, lists_ref, out_ref, table, tiles):
    fill_phases(table, MAIN_ROWS, lax.axis_index("dir") * 16, *sizes)

    def store(i, b, tile):
        out_ref[pl.ds(pl.multiple_of(i * 72 + b * 8, 8), 8), :] = tile

    aggregate(x_ref, tiles, table, MAIN_ROWS, store)
    boxes, entries = lists_ref.shape[0] // 2, lists_ref.shape[1]
    source = lists_ref[:boxes, :]
    used = source >= 0
    at = jnp.where(used, (source + source // boxes) * 8, 0)
    by = jnp.where(used, lists_ref[boxes:, :], OPERATORS) * 16
    out_ref[64:72, :] = jnp.zeros((8, LANES), jnp.float32)
    out_ref[64:72, 0:entries] = at.astype(jnp.float32)
    out_ref[64:72, 32 : 32 + entries] = by.astype(jnp.float32)
    note = out_ref[64:72, :]
    for r in range(1, len(MAIN_ROWS)):
        out_ref[r * 72 + 64 : r * 72 + 72, :] = note


def join_kernel(own_ref, edge_ref, out_ref):
    count = len(EDGE_ROWS)
    for i in range(count):
        out_ref[i * 72 : i * 72 + 64, :] = (
            own_ref[i * 72 : i * 72 + 64, :] + edge_ref[i * 64 : i * 64 + 64, :]
        )
        out_ref[i * 72 + 64 : i * 72 + 72, :] = own_ref[i * 72 + 64 : i * 72 + 72, :]
    out_ref[count * 72 :, :] = own_ref[count * 72 :, :]


def pick_kernel(all_ref, out_ref, block_ref, sem):
    rows = all_ref.shape[1]
    wanted = (lax.axis_index("box") + rows - HALO) % rows
    near = pl.ds(pl.multiple_of(wanted // 8 * 8, 8), 8)
    copy = pltpu.make_async_copy(all_ref.at[:, near, :], block_ref, sem)
    copy.start()
    copy.wait()
    at = wanted % 8

    def eight(i, carry):
        first = pl.multiple_of(i * 8, 8)
        rows = [block_ref[first + n, pl.ds(at, 1), :] for n in range(8)]
        out_ref[pl.ds(first, 8), :] = jnp.concatenate(rows, axis=0)
        return carry

    lax.fori_loop(0, out_ref.shape[0] // 8, eight, 0)


def sort_kernel(row_ref, out_ref):
    count, wide = row_ref.shape
    source = lax.broadcasted_iota(jnp.int32, (wide, wide), 0)
    target = lax.broadcasted_iota(jnp.int32, (wide, wide), 1)
    half = wide // 2
    wanted = jnp.where(target < half, 2 * target, 2 * (target - half) + 1)
    pick = jnp.where(source == wanted, 1.0, 0.0).astype(jnp.bfloat16)
    values = row_ref[...]
    high = values.astype(jnp.bfloat16)
    rest = values - high.astype(jnp.float32)
    middle = rest.astype(jnp.bfloat16)
    low = (rest - middle.astype(jnp.float32)).astype(jnp.bfloat16)
    three = jnp.dot(
        jnp.concatenate([high, middle, low], axis=0), pick, preferred_element_type=jnp.float32
    )
    in_order = three[:count] + three[count : 2 * count] + three[2 * count :]
    for block in range(4):
        part = in_order[:, block * LANES : (block + 1) * LANES]
        out_ref[pl.ds(block, count, stride=8), :] = part
        out_ref[pl.ds(block + 4, count, stride=8), :] = part
    out_ref[count * 8 : count * 8 + 16, :] = jnp.zeros((16, LANES), jnp.float32)


def translate_kernel(entries, x_ref, operator_ref, out_ref, notes, scalars, sems):
    pairs = out_ref.shape[0] // 128
    sub, lane = tile_iota()
    for h in range(pairs):
        at = h * 144 + 64
        first, second = x_ref[at : at + 8, :], x_ref[at + 72 : at + 80, :]
        both = jnp.where(lane < 64, first, pltpu.roll(second, 64, 1))
        notes[h * 8 : h * 8 + 8, :] = both.astype(jnp.int32)

    def copy(h):
        at = pl.ds(h * 8, 8)
        return pltpu.make_async_copy(notes.at[at, :], scalars.at[at, :], sems.at[h])

    for h in range(pairs):
        copy(h).start()
    sign = jnp.where(sub < 4, -1.0, 1.0).astype(jnp.float32)

    for h in range(pairs):
        copy(h).wait()
        for g in range(2):
            for base in (0, 4):
                sums = [[None, None] for _ in range(4)]
                for k in range(entries):
                    for j in range(4):
                        row = h * 8 + base + j
                        at = pl.multiple_of(scalars[row, g * 64 + k], 8)
                        by = pl.multiple_of(scalars[row, g * 64 + 32 + k], 8)
                        pattern = x_ref[pl.ds(at, 8), :]
                        for which in range(2):
                            part = pattern * operator_ref[pl.ds(by + 8 * which, 8), :]
                            total = sums[j][which]
                            sums[j][which] = part if total is None else total + part
                for j in range(4):
                    at = h * 128 + g * 64 + (base + j) * 8
                    out_ref[at : at + 8, :] = sums[j][0] + swap_parts(sums[j][1]) * sign


def shift_sums(b, get_row, table, rows, kids, sign, put):
    plain = [get_row(i, b) for i in range(len(rows))]
    turned = [swap_parts(tile) * sign for tile in plain]
    for p in range(4):
        sums = []
        for which, source in enumerate((plain, turned)):
            product = []
            for i in range(len(rows)):
                at = (i * 4 + p) * 16 + which * 8
                product.append(source[i] * table[at : at + 8, :])
            per_row = []
            for k in kids:
                terms = [(TAP[r - 2 * k], product[i]) for i, r in enumerate(rows) if r - 2 * k in TAP]
                per_row.append(weighted(terms))
            sums.append(per_row)
        for n, k in enumerate(kids):
            put(4 + p, k, sums[0][n] + sums[1][n])
            put(3 - p, k, sums[0][n] - sums[1][n])


def turn_sign():
    sub, _ = tile_iota()
    return jnp.where(sub < 4, -1.0, 1.0).astype(jnp.float32)


def azimuth_back(tiles, base, rows, weights):
    even, odd = [], []
    for part in range(2):
        blocks = [tiles[pl.ds(base + part * 4 + block, rows, stride=8), :] for block in range(4)]
        even.append(jnp.concatenate(blocks[:2], axis=1))
        odd.append(jnp.concatenate(blocks[2:], axis=1))
    mixed = split_dot(jnp.concatenate(odd, axis=0), weights)
    return [even[part] + mixed[part * rows : part * rows + rows] for part in range(2)]


def inner_kernel(r_ref, table, out_ref, tiles):
    boxes, cols = out_ref.shape[1] // 64, out_ref.shape[2]
    weights = azimuth_weights(cols, True)
    sign = turn_sign()

    def get_row(i, b):
        return r_ref[pl.ds(pl.multiple_of(i * 64 + b * 8, 8), 8), :]

    def shift(b, carry):
        def put(c, k, tile):
            tiles[pl.ds(pl.multiple_of(b * 512 + (c * 8 + k) * 8, 8), 8), :] = tile

        shift_sums(b, get_row, table, MAIN_ROWS, tuple(range(8)), sign, put)
        values = azimuth_back(tiles, b * 512, 64, weights)
        for part in range(2):
            out_ref[part, pl.ds(pl.multiple_of(b * 64, 64), 64), :] = values[part]
        return carry

    lax.fori_loop(0, boxes, shift, 0, unroll=2)


def outer_kernel(edge_ref, table, part_ref, out_hbm, out_ref, tiles, sems):
    boxes, cols = out_ref.shape[1] // 64, out_ref.shape[2]
    weights = azimuth_weights(cols, True)
    sign = turn_sign()
    nothing = jnp.zeros((8, LANES), jnp.float32)

    def get_row(i, b):
        return edge_ref[pl.ds(pl.multiple_of(i * 64 + b * 8, 8), 8), :]

    def copy(b):
        at = pl.ds(pl.multiple_of(b * 64, 64), 64)
        return pltpu.make_async_copy(out_ref.at[:, at, :], out_hbm.at[:, at, :], sems.at[b])

    blank = jnp.zeros((4, cols), jnp.float32)

    def box(b, carry):
        def put(c, k, tile):
            tiles[pl.ds(pl.multiple_of(b * 256 + (c * 4 + k - 4) * 8, 8), 8), :] = tile

        for c in range(KIDS):
            put(c, 4, nothing)
        shift_sums(b, get_row, table, EDGE_ROWS, (5, 6, 7), sign, put)
        values = azimuth_back(tiles, b * 256, 32, weights)
        at = pl.ds(pl.multiple_of(b * 64, 64), 64)
        for part in range(2):
            pieces = []
            for c in range(KIDS):
                pieces += [blank, values[part][c * 4 : c * 4 + 4]]
            out_ref[part, at, :] = part_ref[part, at, :] + jnp.concatenate(pieces, axis=0)
        copy(b).start()
        return carry

    lax.fori_loop(0, boxes, box, 0, unroll=8)
    for b in range(boxes):
        copy(b).wait()


def to_next(value, step):
    size = lax.axis_size("dir")
    return lax.ppermute(value, "dir", [(i, (i + step) % size) for i in range(size)])


def call(kernel, outs, scratch, flops, moved, *args, in_hbm=(), out_hbm=False, limit=VMEM, aliases=None):
    whole = pl.BlockSpec(memory_space=pltpu.VMEM)
    far = pl.BlockSpec(memory_space=pltpu.HBM)
    out_specs = [whole] * len(outs) if isinstance(outs, list) else far if out_hbm else whole
    return pl.pallas_call(
        kernel,
        out_shape=outs,
        in_specs=[far if i in in_hbm else whole for i in range(len(args))],
        out_specs=out_specs,
        scratch_shapes=scratch,
        input_output_aliases=aliases or {},
        compiler_params=pltpu.CompilerParams(vmem_limit_bytes=limit),
        cost_estimate=pl.CostEstimate(flops=flops, bytes_accessed=moved, transcendentals=0),
    )(*args)


def on_device(child_patterns, translation, source_list, operator_list):
    parts, boxes, kids, half_rows, cols = child_patterns.shape
    local_rows = 2 * half_rows
    sizes = (local_rows * lax.axis_size("dir"), 2 * cols)
    groups = lax.axis_size("box")
    operators = translation.shape[0]
    f32 = jnp.float32
    shape = jax.ShapeDtypeStruct
    x = child_patterns.reshape(parts, boxes * kids * half_rows, cols)
    work = pltpu.VMEM((boxes * 512 + 8, LANES), f32)
    sems = pltpu.SemaphoreType.DMA((boxes,))
    edge = len(EDGE_ROWS)

    share, edge_table, x = call(
        functools.partial(edge_kernel, sizes),
        [
            shape((edge * boxes * 8, LANES), f32),
            shape((edge * 64, LANES), f32),
            shape(x.shape, f32),
        ],
        [work],
        10**7,
        10**6,
        x,
        aliases={0: 2},
    )
    share, source_list, operator_list = lax.optimization_barrier(
        (share, source_list, operator_list)
    )
    from_last = to_next(share, 1)
    own, main_table = call(
        functools.partial(main_kernel, sizes),
        [shape((local_rows * 72, LANES), f32), shape((local_rows * 64, LANES), f32)],
        [work],
        2 * 10**7,
        4 * 10**6,
        x,
        jnp.concatenate([source_list, operator_list]),
    )
    parent = call(join_kernel, shape(own.shape, f32), [], 10**5, 10**6, own, from_last)

    parent, translation = lax.optimization_barrier((parent, translation))
    place = lax.axis_index("box")
    row = call(
        pick_kernel,
        shape((operators * 2, 2 * cols), f32),
        [pltpu.VMEM((operators * 2, 8, 2 * cols), f32), pltpu.SemaphoreType.DMA],
        2 * 10**7,
        4 * 10**6,
        translation.reshape(operators * 2, local_rows, 2 * cols),
        in_hbm=(0,),
        limit=PICK_VMEM,
    )
    row = jnp.where(place < HALO, to_next(row, 1), row)
    sorted_operators = call(
        sort_kernel, shape(((operators + 1) * 16, LANES), f32), [], 2 * 10**7, 4 * 10**6, row
    )
    patterns = lax.all_to_all(
        parent.reshape(local_rows, 72, LANES), "box", 0, 0, tiled=True
    ).reshape(groups * 72, LANES)
    received = call(
        functools.partial(translate_kernel, source_list.shape[1]),
        shape((groups * 64, LANES), f32),
        [
            pltpu.VMEM((groups * 4, LANES), jnp.int32),
            pltpu.SMEM((groups * 4, LANES), jnp.int32),
            pltpu.SemaphoreType.DMA((groups // 2,)),
        ],
        2 * 10**7,
        2 * 10**6,
        patterns,
        sorted_operators,
    )
    received = received.reshape(groups, 64, LANES)
    received = lax.all_to_all(received, "box", 0, 0, tiled=True)
    received = received.reshape(local_rows * 64, LANES)
    from_next = to_next(received[: edge * 64], -1)
    inner = call(
        inner_kernel, shape(x.shape, f32), [work], 2 * 10**7, 4 * 10**6, received, main_table
    )
    out = call(
        outer_kernel,
        shape(x.shape, f32),
        [pltpu.VMEM(x.shape, f32), pltpu.VMEM((boxes * 256 + 8, LANES), f32), sems],
        10**7,
        2 * 10**6,
        from_next,
        edge_table,
        inner,
        out_hbm=True,
    )
    return out.reshape(child_patterns.shape)


def solution(mesh):
    return jax.shard_map(
        on_device,
        mesh=mesh,
        in_specs=(
            P(None, "box", None, "dir", None),
            P(None, None, "dir", None),
            P("box", None),
            P("box", None),
        ),
        out_specs=P(None, "box", None, "dir", None),
        check_vma=False,
    )
```
